32 devices in a mesh: groups: 2 (over x), expert: 16 (over z, y, core).
Axes of the slice: x: 2, y: 2, z: 4, core: 2. Of those that a mesh axis runs over, the one named last changes fastest.
Arguments:
- hidden: bfloat16 [2, 256, 4096], P(None, ('groups', 'expert')), parts along dimension 1, may hold values from -6 to 6
- queries: bfloat16 [2, 256, 8192], P(None, ('groups', 'expert')), parts along dimension 1
- kv_cache: bfloat16 [2, 256, 128, 2, 512], P(None, ('groups', 'expert')), parts along dimension 1, may hold values from -6 to 6
- lengths: int32 [2, 256], P(None, ('groups', 'expert')), parts along dimension 1, may hold values from 1 to 128, as said below
- routes: int32 [2, 256, 8], P(None, ('groups', 'expert')), parts along dimension 1, may hold values from 0 to 15, all different within a row; in each aligned block of 8 rows (0 to 7, 8 to 15, ..., all dimensions but the last counted through in order) at most 8 rows name the same one
- out_weight: bfloat16 [8192, 4096], P(None, 'expert'), may hold values from -0.0625 to 0.0625
- norm_gain: float32 [4096], replicated, may hold values from 0.5 to 1.5
- router_weight: bfloat16 [4096, 16], replicated, may hold values from -0.09375 to 0.09375
- gate_codes: bfloat16 [16, 4096, 192], P('expert'), may hold values from 0 to 255, as said below
- up_codes: bfloat16 [16, 4096, 192], P('expert'), may hold values from 0 to 255, as said below
- down_codes: bfloat16 [16, 768, 1024], P('expert'), may hold values from 0 to 255, as said below
- codebooks: bfloat16 [16, 3, 256, 4], P('expert'), may hold values from -4 to 4
- gate_up_scale: float32 [16, 2, 768], P('expert'), may hold values from 0.0078125 to 0.03125
- down_scale: float32 [16, 4096], P('expert'), may hold values from 0.018042196 to 0.07216878
Outputs:
- layer_out: bfloat16 [2, 256, 4096], P(None, ('groups', 'expert')), parts along dimension 1
The draws below stay inside these ranges and needn't reach their ends.
There are 2 independent parts, one for each index of `groups`. The reference program is written for one: setup_inputs(seed, part) draws one part's arguments, and reference() takes and returns one part's arrays. A program takes and returns all parts, laid end to end along the dimension named above; an argument that names none is the same for every part. Nothing has to cross between parts.
Inputs may be any that keep to these rules, and one draw needn't show every extreme that they name: `lengths`: at least one sequence of every draw has exactly 128 filled positions. `routes`: A token names 8 different experts; among the sequences of one device in one micro-batch no expert is named more than 8 times, a bound that some block reaches. `gate_codes`: whole numbers. `up_codes`: whole numbers. `down_codes`: whole numbers.
All inputs are finite; a program needn't handle non-finite values.
Results may differ from the reference program's by a relative error of at most 0.0091.
Values may be sent and summed in bfloat16 or wider, within the bound.
No kernel may reach another device: no remote copies, remote signals or barrier semaphores. Data moves between devices by JAX's collectives and lax.ppermute only.
A program may use at most 128 MiB of HBM per device.

```python
import math
import jax
import jax.numpy as jnp
import numpy as np
from jax import lax

D = 4096
FF = 768
HEADS = 64
KV_HEADS = 4
HEAD_DIM = 128
TOPK = 8
CODES = 256
MICRO = 2
ROWS_DEV = 8
KV_LEN = 128
EXPERTS = 16
ROWS = 128
CAP = 8
N_EXPERT = 16


def draw_queries(key, part):
    key = jax.random.fold_in(key, 21)
    first = jax.random.fold_in(key, 0)
    values = jax.random.normal(first, (MICRO, ROWS, HEADS * HEAD_DIM), jnp.float32)
    values = jnp.clip(values, -6.0, 6.0)
    return values.astype(jnp.bfloat16)


def draw_lengths(key, part):
    key = jax.random.fold_in(key, 11)
    first, second, third = jax.random.split(key, 3)
    blocks = ROWS // ROWS_DEV
    ceilings = jax.random.randint(first, (MICRO, blocks, 1), KV_LEN // 4 + 1, KV_LEN + 1)
    fractions = jax.random.randint(second, (MICRO, blocks, ROWS_DEV), 0, 65536)
    spans = 1 + fractions * ceilings // 65536
    flattened = spans.reshape(-1)
    chosen = jax.random.randint(third, (), 0, MICRO * ROWS)
    flattened = flattened.at[chosen].set(KV_LEN)
    return flattened.reshape(MICRO, ROWS).astype(jnp.int32)


def code_table(key, shape):
    return jax.random.randint(key, shape, 0, CODES).astype(jnp.float32).astype(jnp.bfloat16)


def draw_gate_codes(key, part):
    key = jax.random.fold_in(key, 31)
    return code_table(key, (EXPERTS, D, FF // 4))


def draw_up_codes(key, part):
    key = jax.random.fold_in(key, 41)
    return code_table(key, (EXPERTS, D, FF // 4))


def draw_down_codes(key, part):
    key = jax.random.fold_in(key, 51)
    return code_table(key, (EXPERTS, FF, D // 4))


def block_levels(stream_key, shape, pieces, low, top_value):
    def one(dim, shards_of):
        draws = jax.random.uniform(jax.random.fold_in(jax.random.fold_in(stream_key, 6), dim), (shards_of,), jnp.float32, low / len(pieces), top_value / len(pieces))
        return jnp.repeat(jnp.exp(draws), shape[dim] // shards_of).reshape((-1,) + (1,) * (len(shape) - dim - 1))

    level = one(*pieces[0])
    for cut in pieces[1:]:
        level = level * one(*cut)
    return level


def routed_block(rng, own, number, rows, number_of, top, most, slope):
    order = jax.random.permutation(rng, number_of)
    heavy_load, common = shares(number_of, rows * top, most, slope, True), shares(number_of, rows * top, most, slope, False)
    places = jnp.arange(number_of)

    def named(sizes, rotation):
        used = int((sizes > 0).sum())
        fixed = max(1, used // 4)
        moved = fixed + (places - fixed + rotation * (used - fixed)) % max(1, number_of - fixed)
        return jnp.zeros((number_of,), jnp.int32).at[order[jnp.where(places < fixed, places, moved)]].set(jnp.asarray(sizes, jnp.int32))

    sizes = jnp.where(number % 4 == 0, named(heavy_load, number // 4), named(common, number - number // 4 - 1))
    mixed = jax.random.permutation(jax.random.fold_in(own, 3), number_of)
    source_of, taker = mixed[0:number_of // 2 * 2:2], mixed[1:number_of // 2 * 2:2]
    slack = jnp.minimum(sizes[source_of] - 1, most - sizes[taker]) // 2
    slack = jnp.where((source_of == order[0]) | (taker == order[0]) | (sizes[taker] == 0), 0, jnp.maximum(slack, 0))
    moved = jax.random.randint(jax.random.fold_in(own, 4), (number_of // 2,), 0, 1 << 20) % (slack + 1)
    sizes = sizes.at[source_of].add(-moved).at[taker].add(moved)
    items = jnp.searchsorted(jnp.cumsum(sizes), jnp.arange(rows * top), side="right").astype(jnp.int32)
    listing = items.reshape(top, rows).T
    listing = listing[jax.random.permutation(jax.random.fold_in(own, 1), rows)]
    rotation = jax.random.randint(jax.random.fold_in(own, 2), (rows, 1), 0, top)
    return jnp.take_along_axis(listing, (jnp.arange(top)[None, :] + rotation) % top, axis=1)


def shares(amount, total, most, slope, full):
    loads = [(1 << 20) // math.isqrt(rank ** slope) + 1 for rank in range(1, amount + 1)]
    largest = most if full else min(most, max(-(-total // amount), total * loads[0] // sum(loads)))
    least = 1 if total - largest >= amount - 1 else 0
    counts, spare = [largest] + [least] * (amount - 1), total - largest - least * (amount - 1)
    while spare > 0:
        free = [i for i in range(1, amount) if counts[i] < largest] or [i for i in range(1, amount) if counts[i] < most]
        mass, remaining = sum([loads[i] for i in free]), spare
        for i in free:
            extra = min(most - counts[i], max(1, remaining * loads[i] // mass), spare)
            counts[i] = counts[i] + extra
            spare = spare - extra
    return np.array(counts)


def gaussian(rng, extent, deviation, reach, shards=(), kind=jnp.bfloat16):
    drawn = jax.random.normal(rng, extent, jnp.float32) * deviation
    if len(shards) > 0:
        drawn = block_levels(rng, extent, shards, -0.22, 0.18) * drawn
    return jnp.clip(drawn, min=-reach, max=reach).astype(kind)


def setup_inputs(seed: int = 0, part: int = 0) -> dict:
    key_of = jax.random.split(jax.random.key(seed), 15)
    part_keys = jax.random.split(jax.random.fold_in(key_of[14], part), 15)
    hidden = gaussian(part_keys[0], (MICRO, ROWS, D), 1.0, 6.0, ((1, 16),))
    queries = draw_queries(jax.random.fold_in(jax.random.fold_in(key_of[14], part), 71), part)
    kv_cache = gaussian(part_keys[2], (MICRO, ROWS, KV_LEN, 2, KV_HEADS * HEAD_DIM), 1.0, 6.0, ((1, 16),))
    lengths = draw_lengths(jax.random.fold_in(jax.random.fold_in(key_of[14], part), 71), part)
    routes_keys = jax.random.split(jax.random.fold_in(part_keys[4], 1), MICRO * ROWS // ROWS_DEV)
    routes_turns = jax.random.permutation(jax.random.fold_in(part_keys[4], 3), MICRO * ROWS // ROWS_DEV)
    routes = jax.vmap(lambda own, number: routed_block(jax.random.fold_in(part_keys[4], 2), own, number, ROWS_DEV, EXPERTS, TOPK, CAP, 2))(routes_keys, routes_turns).reshape((MICRO, ROWS, TOPK))
    out_weight = gaussian(key_of[5], (HEADS * HEAD_DIM, D), (HEADS * HEAD_DIM) ** -0.5, 0.0625, ((1, 16),))
    norm_gain = jnp.clip(1.0 + 0.1 * jax.random.normal(key_of[6], (D,), jnp.float32), 0.5, 1.5)
    router_weight = gaussian(key_of[7], (D, EXPERTS), D ** -0.5, 0.09375)
    gate_codes = draw_gate_codes(jax.random.fold_in(key_of[14], 71), part)
    up_codes = draw_up_codes(jax.random.fold_in(key_of[14], 71), part)
    down_codes = draw_down_codes(jax.random.fold_in(key_of[14], 71), part)
    codebooks = gaussian(key_of[11], (EXPERTS, 3, CODES, 4), 1.0, 4.0, ((0, 16),))
    gate_up_scale = jnp.clip(jnp.exp(math.log(0.03125) - 1.3862944 * jax.random.uniform(key_of[12], (EXPERTS, 2, FF), jnp.float32) ** block_levels(key_of[12], (EXPERTS, 2, FF), ((0, 16),), -0.2, 0.2)), 0.0078125, 0.03125)
    down_scale = jnp.clip(jnp.exp(math.log(0.07216878) - 1.3862944 * jax.random.uniform(key_of[13], (EXPERTS, D), jnp.float32) ** block_levels(key_of[13], (EXPERTS, D), ((0, 16),), -0.2, 0.2)), 0.018042196, 0.07216878)
    return dict(hidden=hidden, queries=queries, kv_cache=kv_cache, lengths=lengths, routes=routes, out_weight=out_weight, norm_gain=norm_gain, router_weight=router_weight, gate_codes=gate_codes, up_codes=up_codes, down_codes=down_codes, codebooks=codebooks, gate_up_scale=gate_up_scale, down_scale=down_scale)


def attend(query_rows, cache_rows, length):
    row_count, positions = (cache_rows.shape[0], cache_rows.shape[1])
    query_heads = query_rows.astype(jnp.float32).reshape(row_count, KV_HEADS, HEADS // KV_HEADS, HEAD_DIM)
    key_rows = cache_rows[:, :, 0].astype(jnp.float32).reshape(row_count, positions, KV_HEADS, HEAD_DIM)
    value_rows = cache_rows[:, :, 1].astype(jnp.float32).reshape(row_count, positions, KV_HEADS, HEAD_DIM)
    scores = jnp.einsum('rgqd,rlgd->rgql', query_heads, key_rows) * HEAD_DIM ** (-0.5)
    visible = jnp.arange(positions, dtype=jnp.int32)[None, :] < length[:, None]
    scores = jnp.where(visible[:, None, None, :], scores, -1e+30)
    row_max = lax.optimization_barrier(jnp.max(scores, axis=-1, keepdims=True))
    weights = jnp.exp(scores - row_max)
    weights = (weights / lax.optimization_barrier(jnp.sum(weights, axis=-1, keepdims=True))).astype(jnp.bfloat16)
    mixture = jnp.einsum('rgql,rlgd->rgqd', weights.astype(jnp.float32), value_rows)
    return mixture.reshape(row_count, HEADS * HEAD_DIM).astype(jnp.bfloat16)

def rms_norm(stream, gain):
    values = stream.astype(jnp.float32)
    return (values * lax.rsqrt(lax.optimization_barrier(jnp.mean(values * values, axis=-1, keepdims=True)) + 1e-06) * gain).astype(jnp.bfloat16)

def slot_numbers(choices, experts):
    flattened = choices.reshape(-1)
    matches = (flattened[:, None] == jnp.arange(experts, dtype=jnp.int32)[None, :]).astype(jnp.int32)
    earlier = jnp.cumsum(matches, axis=0) - matches
    return lax.optimization_barrier(jnp.sum(earlier * matches, axis=1)).reshape(choices.shape)

def expand(code_block, codebook, scales):
    row_total, columns = code_block.shape
    picked = codebook.astype(jnp.float32)[code_block.astype(jnp.int32)]
    picked = jnp.transpose(picked, (0, 2, 1)).reshape(row_total, 4 * columns)
    return (picked * scales[None, :]).astype(jnp.bfloat16)

def experts_apply(rows_in, w_gate, w_up, w_down):
    gate_vals = jnp.dot(rows_in, w_gate, preferred_element_type=jnp.float32)
    up_vals = jnp.dot(rows_in, w_up, preferred_element_type=jnp.float32)
    inner = (jax.nn.silu(gate_vals) * up_vals).astype(jnp.bfloat16)
    return jnp.dot(inner, w_down, preferred_element_type=jnp.float32).astype(jnp.bfloat16)

def reference(hidden, queries, kv_cache, lengths, routes, out_weight, norm_gain, router_weight, gate_codes, up_codes, down_codes, codebooks, gate_up_scale, down_scale):
    experts = N_EXPERT
    streams = []
    normed = []
    for micro_idx in range(MICRO):
        attended = attend(queries[micro_idx], kv_cache[micro_idx], lengths[micro_idx])
        projected = jnp.dot(attended, out_weight, preferred_element_type=jnp.float32).astype(jnp.bfloat16)
        stream = (hidden[micro_idx].astype(jnp.float32) + projected.astype(jnp.float32)).astype(jnp.bfloat16)
        streams.append(stream)
        normed.append(rms_norm(stream, norm_gain))
    streams = jnp.stack(streams)
    tokens = jnp.stack(normed)
    logits = jnp.einsum('mrd,de->mre', tokens.astype(jnp.float32), router_weight.astype(jnp.float32))
    expert_hot = routes[..., None] == jnp.arange(experts, dtype=jnp.int32)
    chosen = lax.optimization_barrier(jnp.sum(jnp.where(expert_hot, logits[:, :, None, :], 0.0), axis=-1))
    gate_weights = jax.nn.softmax(chosen, axis=-1).astype(jnp.bfloat16)
    choices = routes.reshape(MICRO, experts, ROWS_DEV, TOPK)
    slots = jax.vmap(jax.vmap(lambda blocks: slot_numbers(blocks, experts)))(choices)
    source_ids = jnp.broadcast_to(jnp.arange(experts, dtype=jnp.int32)[None, :, None, None], choices.shape)
    micro_ids = jnp.broadcast_to(jnp.arange(MICRO, dtype=jnp.int32)[:, None, None, None], choices.shape)
    spread = jnp.broadcast_to(tokens.reshape(MICRO, experts, ROWS_DEV, 1, D), (MICRO, experts, ROWS_DEV, TOPK, D))
    buffer = jnp.zeros((experts, experts, MICRO, CAP, D), jnp.bfloat16).at[choices, source_ids, micro_ids, slots].set(spread)

    def one_expert(operands):
        gate_part, up_part, down_part, book_part, gate_up_part, down_part_scale, rows_in = operands
        w_gate = expand(gate_part, book_part[0], gate_up_part[0])
        w_up = expand(up_part, book_part[1], gate_up_part[1])
        w_down = expand(down_part, book_part[2], down_part_scale)
        return experts_apply(rows_in.reshape(-1, D), w_gate, w_up, w_down).reshape(rows_in.shape)
    results = lax.map(one_expert, (gate_codes, up_codes, down_codes, codebooks, gate_up_scale, down_scale, buffer))
    picked = results[choices, source_ids, micro_ids, slots].astype(jnp.float32)
    weighted = gate_weights.astype(jnp.float32).reshape(MICRO, experts, ROWS_DEV, TOPK, 1) * picked
    mixture = lax.optimization_barrier(jnp.sum(weighted, axis=3)).reshape(MICRO, ROWS, D)
    return (streams.astype(jnp.float32) + mixture).astype(jnp.bfloat16)
```

```python
import functools

import jax
import jax.numpy as jnp
from jax import lax
from jax.experimental import pallas as pl
from jax.experimental.pallas import tpu as pltpu
from jax.sharding import PartitionSpec as P

LANES = 128
KV_HEADS = 4
HEAD_DIM = 128
VMEM = 60 << 20


def attend_kernel(micro, span, kv_heads, len_ref, q_ref, kv_ref, out_ref, q_scr, o_scr):
    step = pl.program_id(0)
    rows, width = q_ref.shape
    heads = width // HEAD_DIM
    per_group = heads // kv_heads
    positions = kv_ref.shape[1]

    @pl.when(step == 0)
    def _():
        for h in range(heads):
            q_scr[h] = q_ref[:, h * HEAD_DIM : (h + 1) * HEAD_DIM].astype(jnp.float32)

    column = lax.broadcasted_iota(jnp.int32, (heads, 2 * positions), 1)
    is_key = column % 2 == 0
    blocks, weights = [], []
    for i in range(span):
        row = step * span + i
        parts = [
            kv_ref[i, :, :, g * HEAD_DIM : (g + 1) * HEAD_DIM].reshape(2 * positions, HEAD_DIM)
            for g in range(kv_heads)
        ]
        blocks.append(parts)
        scores = jnp.concatenate(
            [
                lax.dot_general(
                    q_scr[g * per_group : (g + 1) * per_group, row, :].astype(jnp.bfloat16),
                    parts[g],
                    (((1,), (1,)), ((), ())),
                    preferred_element_type=jnp.float32,
                )
                for g in range(kv_heads)
            ],
            axis=0,
        ) * HEAD_DIM ** (-0.5)
        visible = is_key & (column < 2 * len_ref[micro, row])
        scores = jnp.where(visible, scores, -1e30)
        raised = jnp.exp(scores - jnp.max(scores, axis=-1, keepdims=True))
        raised = raised / jnp.sum(raised, axis=-1, keepdims=True)
        weights.append(pltpu.roll(raised, 1, 1).astype(jnp.bfloat16))
    for i in range(span):
        row = step * span + i
        for g in range(kv_heads):
            o_scr[g * per_group : (g + 1) * per_group, row, :] = jnp.dot(
                weights[i][g * per_group : (g + 1) * per_group],
                blocks[i][g],
                preferred_element_type=jnp.float32,
            )

    @pl.when(step == pl.num_programs(0) - 1)
    def _():
        for h in range(heads):
            out_ref[:, h * HEAD_DIM : (h + 1) * HEAD_DIM] = o_scr[h].astype(jnp.bfloat16)


def attend(queries, kv_cache, lengths, micro):
    _, rows, width = queries.shape
    heads = width // HEAD_DIM
    span = 4 if rows % 4 == 0 else 1
    kv_shape = kv_cache.shape[2:]
    return pl.pallas_call(
        functools.partial(attend_kernel, micro, span, KV_HEADS),
        grid_spec=pltpu.PrefetchScalarGridSpec(
            num_scalar_prefetch=1,
            grid=(rows // span,),
            in_specs=[
                pl.BlockSpec((None, rows, width), lambda r, n: (micro, 0, 0)),
                pl.BlockSpec((None, span) + kv_shape, lambda r, n: (micro, r, 0, 0, 0)),
            ],
            out_specs=pl.BlockSpec((rows, width), lambda r, n: (0, 0)),
            scratch_shapes=[pltpu.VMEM((heads, rows, HEAD_DIM), jnp.float32)] * 2,
        ),
        out_shape=jax.ShapeDtypeStruct((rows, width), jnp.bfloat16),
        name="attend",
        compiler_params=pltpu.CompilerParams(vmem_limit_bytes=VMEM),
        cost_estimate=pl.CostEstimate(
            flops=rows * width * 4 * 256, bytes_accessed=rows << 18, transcendentals=0
        ),
    )(lengths, queries, kv_cache)


def expand_kernel(stacked, table_ref, code_ref, out_ref):
    rows, columns = code_ref.shape
    tile = 16
    tables = [jnp.broadcast_to(table_ref[i : i + 1], (tile, LANES)) for i in range(8)]

    def one(i, lane):
        at = pl.ds(pl.multiple_of(i * tile, tile), tile)
        codes = code_ref[at, lane * LANES : (lane + 1) * LANES]
        codes = codes.astype(jnp.float32).astype(jnp.int32)
        upper = codes >= LANES
        low = jnp.bitwise_and(codes, LANES - 1)

        def take(table):
            return jnp.take_along_axis(table, low, axis=1, mode="promise_in_bounds")

        for q in range(4):
            value = jnp.where(upper, take(tables[2 * q + 1]), take(tables[2 * q]))
            value = value.astype(jnp.bfloat16)
            if stacked:
                out_ref[q, at, lane * LANES : (lane + 1) * LANES] = value
            else:
                first = q * columns + lane * LANES
                out_ref[at, first : first + LANES] = value

    for lane in range(columns // LANES):

        def body(i, _, lane=lane):
            one(i, lane)
            return 0

        lax.fori_loop(0, rows // tile, body, 0, unroll=rows // tile if rows // tile <= 12 else 8)


def expand(table, codes, stacked):
    rows, columns = codes.shape
    if stacked:
        block = 512
        grid = (columns // block,)
        code_spec = pl.BlockSpec((rows, block), lambda b: (0, b))
        out_spec = pl.BlockSpec((4, rows, block), lambda b: (0, 0, b))
        out_shape = (4, rows, columns)
    else:
        block = 128
        grid = (rows // block,)
        code_spec = pl.BlockSpec((block, columns), lambda b: (b, 0))
        out_spec = pl.BlockSpec((block, 4 * columns), lambda b: (b, 0))
        out_shape = (rows, 4 * columns)
    out = pl.pallas_call(
        functools.partial(expand_kernel, stacked),
        grid=grid,
        in_specs=[pl.BlockSpec((8, LANES), lambda b: (0, 0)), code_spec],
        out_specs=out_spec,
        out_shape=jax.ShapeDtypeStruct(out_shape, jnp.bfloat16),
        name="expand",
        compiler_params=pltpu.CompilerParams(vmem_limit_bytes=VMEM),
        cost_estimate=pl.CostEstimate(
            flops=rows * columns * 8000, bytes_accessed=10 * rows * columns, transcendentals=0
        ),
    )(table, codes)
    return out.reshape(4 * rows, columns) if stacked else out


def project_kernel(blocks, me_ref, att_ref, weight_ref, hidden_ref, out_ref, acc_ref):
    step = pl.program_id(0)
    shards, rows, depth = att_ref.shape

    @pl.when(step == 0)
    def _():
        acc_ref[...] = jnp.zeros_like(acc_ref)

    product = jnp.dot(
        att_ref[...].reshape(shards * rows, depth),
        weight_ref[...],
        preferred_element_type=jnp.float32,
    )
    acc_ref[...] += product.reshape(acc_ref.shape)

    @pl.when(step == pl.num_programs(0) - 1)
    def _():
        me = me_ref[0]
        for p in range(shards):
            source = me ^ blocks[p]
            projected = acc_ref[p].astype(jnp.bfloat16).astype(jnp.float32)
            out_ref[source] = (hidden_ref[source].astype(jnp.float32) + projected).astype(
                jnp.bfloat16
            )


def project(me, attended, out_weight, hidden_columns, blocks):
    shards, rows, depth = attended.shape
    columns = out_weight.shape[1]
    block = 2048
    return pl.pallas_call(
        functools.partial(project_kernel, blocks),
        grid_spec=pltpu.PrefetchScalarGridSpec(
            num_scalar_prefetch=1,
            grid=(depth // block,),
            in_specs=[
                pl.BlockSpec((shards, rows, block), lambda k, n: (0, 0, k)),
                pl.BlockSpec((block, columns), lambda k, n: (k, 0)),
                pl.BlockSpec((shards, rows, columns), lambda k, n: (0, 0, 0)),
            ],
            out_specs=pl.BlockSpec((shards, rows, columns), lambda k, n: (0, 0, 0)),
            scratch_shapes=[pltpu.VMEM((shards, rows, columns), jnp.float32)],
        ),
        out_shape=jax.ShapeDtypeStruct((shards, rows, columns), jnp.bfloat16),
        name="project",
        compiler_params=pltpu.CompilerParams(vmem_limit_bytes=VMEM),
        cost_estimate=pl.CostEstimate(
            flops=2 * shards * rows * depth * columns,
            bytes_accessed=2 * depth * columns,
            transcendentals=0,
        ),
    )(me, attended, out_weight, hidden_columns)


def experts_kernel(
    blocks,
    me_ref,
    stream_ref,
    gain_ref,
    router_ref,
    hot_ref,
    gate_ref,
    up_ref,
    down_ref,
    gu_scale_ref,
    down_scale_ref,
    out_ref,
    own_ref,
    token_scr,
    weight_scr,
    acc_ref,
):
    step = pl.program_id(0)
    pieces, shards, rows, columns = stream_ref.shape
    total, width = token_scr.shape
    me = me_ref[0]

    @pl.when(step == 0)
    def _():
        squares = jnp.zeros((total, columns), jnp.float32)
        for p in range(pieces):
            value = stream_ref[p].reshape(total, columns).astype(jnp.float32)
            squares += value * value
        mean = jnp.sum(squares, axis=-1, keepdims=True) / width
        inverse = lax.rsqrt(mean + 1e-06)
        for p in range(pieces):
            at = pl.ds(0, columns)
            if pieces > 1:
                at = pl.ds(pl.multiple_of((me ^ blocks[p]) * columns, columns), columns)
            value = stream_ref[p].reshape(total, columns)
            own_ref[:, at] = stream_ref[p, me]
            token_scr[:, at] = (value.astype(jnp.float32) * inverse * gain_ref[:, at]).astype(
                jnp.bfloat16
            )
        logits = lax.dot_general(
            token_scr[...],
            router_ref[...],
            (((1,), (1,)), ((), ())),
            preferred_element_type=jnp.float32,
        )
        hot = hot_ref[...].astype(jnp.float32) > 0.5
        logits = jnp.where(hot, logits, -1e30)
        raised = jnp.where(hot, jnp.exp(logits - jnp.max(logits, axis=-1, keepdims=True)), 0.0)
        raised = raised / jnp.sum(raised, axis=-1, keepdims=True)
        mine = lax.broadcasted_iota(jnp.int32, raised.shape, 1) == me
        weight = jnp.sum(jnp.where(mine, raised, 0.0), axis=-1, keepdims=True)
        weight = weight.astype(jnp.bfloat16).astype(jnp.float32)
        weight_scr[...] = jnp.broadcast_to(weight, (total, LANES)).reshape(weight_scr.shape)
        acc_ref[...] = jnp.zeros_like(acc_ref)

    nt = (((1,), (1,)), ((), ()))
    tokens = token_scr[...]
    gate = lax.dot_general(tokens, gate_ref[...], nt, preferred_element_type=jnp.float32)
    up = lax.dot_general(tokens, up_ref[...], nt, preferred_element_type=jnp.float32)
    gate = gate * gu_scale_ref[0:1, :]
    up = up * gu_scale_ref[1:2, :]
    inner = (gate / (1.0 + jnp.exp(-gate)) * up).astype(jnp.bfloat16)
    piece = 1024
    for c in range(width // piece):
        at = slice(c * piece, (c + 1) * piece)
        part = jnp.dot(inner, down_ref[:, at], preferred_element_type=jnp.float32)
        acc_ref[:, :, at] += part.reshape(shards, rows, piece)

    @pl.when(step == pl.num_programs(0) - 1)
    def _():
        for p in range(shards):
            source = me ^ blocks[p]
            value = (acc_ref[source] * down_scale_ref[...]).astype(jnp.bfloat16)
            value = value.astype(jnp.float32) * weight_scr[source][:, 0:1]
            out_ref[p] = value.astype(jnp.bfloat16)


def run_experts(me, streams, gain, router, hot, gate, up, down, gu_scale, down_scale, blocks):
    pieces, shards, rows, columns = streams.shape
    hidden_units, width = gate.shape
    total = shards * rows
    block = 256
    full = lambda f, n: (0, 0)
    return pl.pallas_call(
        functools.partial(experts_kernel, blocks),
        grid_spec=pltpu.PrefetchScalarGridSpec(
            num_scalar_prefetch=1,
            grid=(hidden_units // block,),
            in_specs=[
                pl.BlockSpec(streams.shape, lambda f, n: (0, 0, 0, 0)),
                pl.BlockSpec((1, width), full),
                pl.BlockSpec(router.shape, full),
                pl.BlockSpec(hot.shape, full),
                pl.BlockSpec((block, width), lambda f, n: (f, 0)),
                pl.BlockSpec((block, width), lambda f, n: (f, 0)),
                pl.BlockSpec((block, width), lambda f, n: (f, 0)),
                pl.BlockSpec((2, block), lambda f, n: (0, f)),
                pl.BlockSpec((1, width), full),
            ],
            out_specs=[
                pl.BlockSpec((shards, rows, width), lambda f, n: (0, 0, 0)),
                pl.BlockSpec((rows, width), full),
            ],
            scratch_shapes=[
                pltpu.VMEM((total, width), jnp.bfloat16),
                pltpu.VMEM((shards, rows, LANES), jnp.float32),
                pltpu.VMEM((shards, rows, width), jnp.float32),
            ],
        ),
        out_shape=[
            jax.ShapeDtypeStruct((shards, rows, width), jnp.bfloat16),
            jax.ShapeDtypeStruct((rows, width), jnp.bfloat16),
        ],
        name="experts",
        compiler_params=pltpu.CompilerParams(vmem_limit_bytes=VMEM),
        cost_estimate=pl.CostEstimate(
            flops=6 * total * width * hidden_units,
            bytes_accessed=6 * width * hidden_units,
            transcendentals=0,
        ),
    )(me, streams, gain, router, hot, gate, up, down, gu_scale, down_scale)


def swap(value, bit, count):
    return lax.ppermute(value, "expert", [(i, i ^ bit) for i in range(count)])


def gather_all(value, count):
    bits = [1 << b for b in reversed(range(count.bit_length() - 1))]
    if len(bits) >= 2:
        far = swap(value, bits[0], count)
        near = swap(value, bits[1], count)
        both = swap(far, bits[1], count)
        held, bits = jnp.stack([value, far, near, both]), bits[2:]
    else:
        held = value[None]
    for bit in bits:
        held = jnp.concatenate([held, swap(held, bit, count)])
    return held


def reduce_own(parts, count):
    for bit in [1 << b for b in range(count.bit_length() - 1)]:
        half = parts.shape[0] // 2
        other = swap(parts[half:], bit, count)
        total = parts[:half].astype(jnp.float32) + other.astype(jnp.float32)
        parts = total if half == 1 else total.astype(jnp.bfloat16)
    return parts[0]


def body(
    hidden,
    queries,
    kv_cache,
    lengths,
    routes,
    out_weight,
    norm_gain,
    router_weight,
    gate_codes,
    up_codes,
    down_codes,
    codebooks,
    gate_up_scale,
    down_scale,
):
    micro_count, rows, width = hidden.shape
    count = lax.axis_size("expert")
    me = lax.axis_index("expert").astype(jnp.int32)
    me_list = me.reshape(1)
    columns = out_weight.shape[1]
    width_bits = count.bit_length() - 1
    blocks = tuple(
        sum(((p >> b) & 1) << (width_bits - 1 - b) for b in range(width_bits)) for p in range(count)
    )

    hot = (routes[..., None] == jnp.arange(count, dtype=jnp.int32)).any(axis=2)
    lead = hidden.reshape(micro_count, rows, count, columns).transpose(2, 0, 1, 3)
    tail = jnp.broadcast_to(hot.astype(jnp.bfloat16)[None], (count,) + hot.shape)
    packed = lax.all_to_all(
        jnp.concatenate([lead, tail], axis=-1), "expert", split_axis=0, concat_axis=0, tiled=True
    )
    hidden_columns = packed[..., :columns]
    hot_all = packed[..., columns:]

    tables = codebooks[0].astype(jnp.float32).transpose(0, 2, 1).reshape(3, 8, LANES)
    gathered = [
        gather_all(attend(queries, kv_cache, lengths, m), count) for m in range(micro_count)
    ]
    gate = expand(tables[0], gate_codes[0].T, True)
    up = expand(tables[1], up_codes[0].T, True)
    down = expand(tables[2], down_codes[0], False)

    outputs = []
    for m in range(micro_count):
        stream = project(me_list, gathered[m], out_weight, hidden_columns[:, m], blocks)
        streams = gather_all(stream, count)
        if columns % LANES:
            order = jnp.arange(count, dtype=jnp.int32)
            place = jnp.asarray(blocks, jnp.int32)
            inverse = jnp.argsort(place)
            streams = streams[inverse[order ^ me]]
            streams = streams.transpose(1, 2, 0, 3).reshape(1, count, rows, width)
        parts, own = run_experts(
            me_list,
            streams,
            norm_gain.reshape(1, width),
            router_weight.T,
            hot_all[:, m].reshape(count * rows, count),
            gate,
            up,
            down,
            gate_up_scale[0],
            down_scale,
            blocks,
        )
        mixture = reduce_own(parts, count)
        outputs.append((own.astype(jnp.float32) + mixture).astype(jnp.bfloat16))
    return jnp.stack(outputs)


def solution(mesh):
    in_specs = (
        P(None, ("groups", "expert"), None),
        P(None, ("groups", "expert"), None),
        P(None, ("groups", "expert"), None, None, None),
        P(None, ("groups", "expert")),
        P(None, ("groups", "expert"), None),
        P(None, "expert"),
        P(),
        P(),
        P("expert", None, None),
        P("expert", None, None),
        P("expert", None, None),
        P("expert", None, None, None),
        P("expert", None, None),
        P("expert", None),
    )
    out_specs = P(None, ("groups", "expert"), None)
    return jax.shard_map(body, mesh=mesh, in_specs=in_specs, out_specs=out_specs, check_vma=False)
```

```python
import functools

import jax
import jax.numpy as jnp
from jax import lax
from jax.experimental import pallas as pl
from jax.experimental.pallas import tpu as pltpu
from jax.sharding import PartitionSpec as P

LANES = 128
KV_HEADS = 4
HEAD_DIM = 128
MIB = 1 << 20


def attend_kernel(micro, span, kv_heads, len_ref, q_ref, kv_ref, out_ref, q_scr, o_scr):
    step = pl.program_id(0)
    rows, width = q_ref.shape
    heads = width // HEAD_DIM
    per_group = heads // kv_heads
    positions = kv_ref.shape[1]

    @pl.when(step == 0)
    def _():
        for h in range(heads):
            q_scr[h] = q_ref[:, h * HEAD_DIM : (h + 1) * HEAD_DIM].astype(jnp.float32)

    column = lax.broadcasted_iota(jnp.int32, (heads, 2 * positions), 1)
    is_key = column % 2 == 0
    blocks, weights = [], []
    for i in range(span):
        row = step * span + i
        parts = [
            kv_ref[i, :, :, g * HEAD_DIM : (g + 1) * HEAD_DIM].reshape(2 * positions, HEAD_DIM)
            for g in range(kv_heads)
        ]
        blocks.append(parts)
        scores = jnp.concatenate(
            [
                lax.dot_general(
                    q_scr[g * per_group : (g + 1) * per_group, row, :].astype(jnp.bfloat16),
                    parts[g],
                    (((1,), (1,)), ((), ())),
                    preferred_element_type=jnp.float32,
                )
                for g in range(kv_heads)
            ],
            axis=0,
        ) * HEAD_DIM ** (-0.5)
        visible = is_key & (column < 2 * len_ref[micro, row])
        scores = jnp.where(visible, scores, -1e30)
        raised = jnp.exp(scores - jnp.max(scores, axis=-1, keepdims=True))
        raised = raised / jnp.sum(raised, axis=-1, keepdims=True)
        weights.append(pltpu.roll(raised, 1, 1).astype(jnp.bfloat16))
    for i in range(span):
        row = step * span + i
        for g in range(kv_heads):
            o_scr[g * per_group : (g + 1) * per_group, row, :] = jnp.dot(
                weights[i][g * per_group : (g + 1) * per_group],
                blocks[i][g],
                preferred_element_type=jnp.float32,
            )

    @pl.when(step == pl.num_programs(0) - 1)
    def _():
        for h in range(heads):
            out_ref[:, h * HEAD_DIM : (h + 1) * HEAD_DIM] = o_scr[h].astype(jnp.bfloat16)


def attend(queries, kv_cache, lengths, micro):
    _, rows, width = queries.shape
    heads = width // HEAD_DIM
    span = 4 if rows % 4 == 0 else 1
    kv_shape = kv_cache.shape[2:]
    return pl.pallas_call(
        functools.partial(attend_kernel, micro, span, KV_HEADS),
        grid_spec=pltpu.PrefetchScalarGridSpec(
            num_scalar_prefetch=1,
            grid=(rows // span,),
            in_specs=[
                pl.BlockSpec((None, rows, width), lambda r, n: (micro, 0, 0)),
                pl.BlockSpec((None, span) + kv_shape, lambda r, n: (micro, r, 0, 0, 0)),
            ],
            out_specs=pl.BlockSpec((rows, width), lambda r, n: (0, 0)),
            scratch_shapes=[pltpu.VMEM((heads, rows, HEAD_DIM), jnp.float32)] * 2,
        ),
        out_shape=jax.ShapeDtypeStruct((rows, width), jnp.bfloat16),
        name="attend",
        compiler_params=pltpu.CompilerParams(vmem_limit_bytes=16 * MIB),
        cost_estimate=pl.CostEstimate(
            flops=rows * width * 4 * 256, bytes_accessed=rows << 18, transcendentals=0
        ),
    )(lengths, queries, kv_cache)


def expand_kernel(stacked, table_ref, code_ref, *rest):
    out_ref = rest[-1]
    rows, columns = code_ref.shape
    tile = 16
    tables = [jnp.broadcast_to(table_ref[i : i + 1], (tile, LANES)) for i in range(8)]

    def one(i, lane):
        at = pl.ds(pl.multiple_of(i * tile, tile), tile)
        codes = code_ref[at, lane * LANES : (lane + 1) * LANES]
        codes = codes.astype(jnp.float32).astype(jnp.int32)
        upper = codes >= LANES
        low = jnp.bitwise_and(codes, LANES - 1)

        def take(table):
            return jnp.take_along_axis(table, low, axis=1, mode="promise_in_bounds")

        for q in range(4):
            value = jnp.where(upper, take(tables[2 * q + 1]), take(tables[2 * q]))
            value = value.astype(jnp.bfloat16)
            if stacked:
                out_ref[q, at, lane * LANES : (lane + 1) * LANES] = value
            else:
                first = q * columns + lane * LANES
                out_ref[at, first : first + LANES] = value

    for lane in range(columns // LANES):

        def body(i, _, lane=lane):
            one(i, lane)
            return 0

        lax.fori_loop(0, rows // tile, body, 0, unroll=rows // tile if rows // tile <= 12 else 8)


def expand(table, codes, stacked, after=()):
    rows, columns = codes.shape
    if stacked:
        block = 512
        grid = (columns // block,)
        code_spec = pl.BlockSpec((rows, block), lambda b: (0, b))
        out_spec = pl.BlockSpec((4, rows, block), lambda b: (0, 0, b))
        out_shape = (4, rows, columns)
    else:
        block = 128
        grid = (rows // block,)
        code_spec = pl.BlockSpec((block, columns), lambda b: (b, 0))
        out_spec = pl.BlockSpec((block, 4 * columns), lambda b: (b, 0))
        out_shape = (rows, 4 * columns)
    out = pl.pallas_call(
        functools.partial(expand_kernel, stacked),
        grid=grid,
        in_specs=[pl.BlockSpec((8, LANES), lambda b: (0, 0)), code_spec]
        + [pl.BlockSpec(memory_space=pl.ANY) for _ in after],
        out_specs=out_spec,
        out_shape=jax.ShapeDtypeStruct(out_shape, jnp.bfloat16),
        name="expand",
        compiler_params=pltpu.CompilerParams(vmem_limit_bytes=10 * MIB),
        cost_estimate=pl.CostEstimate(
            flops=rows * columns * 8000, bytes_accessed=10 * rows * columns, transcendentals=0
        ),
    )(table, codes, *after)
    return out.reshape(4 * rows, columns) if stacked else out


def project_kernel(masks, counts, me_ref, *refs):
    pieces, refs = refs[: len(masks)], refs[len(masks) :]
    weight_ref, hidden_ref = refs[:2]
    out_refs, acc_ref = refs[2:-1], refs[-1]
    step = pl.program_id(0)
    depth = weight_ref.shape[0]

    @pl.when(step == 0)
    def _():
        acc_ref[...] = jnp.zeros_like(acc_ref)

    rows_in = jnp.concatenate([ref[...].reshape(-1, depth) for ref in pieces], axis=0)
    product = jnp.dot(rows_in, weight_ref[...], preferred_element_type=jnp.float32)
    acc_ref[...] += product.reshape(acc_ref.shape)

    @pl.when(step == pl.num_programs(0) - 1)
    def _():
        me = me_ref[0]
        at = 0
        for mask_list, m in zip(masks, counts):
            for mask in mask_list:
                source = me ^ mask
                projected = acc_ref[at].astype(jnp.bfloat16).astype(jnp.float32)
                out_refs[m][source] = (
                    hidden_ref[source, m].astype(jnp.float32) + projected
                ).astype(jnp.bfloat16)
                at += 1


def project(me, gathered, out_weight, hidden_columns):
    pieces = [array for chain in gathered for array, _ in chain]
    masks = tuple(mask for chain in gathered for _, mask in chain)
    counts = tuple(m for m, chain in enumerate(gathered) for _ in chain)
    shards, micro_count, rows, columns = hidden_columns.shape
    depth = out_weight.shape[0]
    block = 2048
    return pl.pallas_call(
        functools.partial(project_kernel, masks, counts),
        grid_spec=pltpu.PrefetchScalarGridSpec(
            num_scalar_prefetch=1,
            grid=(depth // block,),
            in_specs=[
                pl.BlockSpec((piece.shape[0], rows, block), lambda k, n: (0, 0, k))
                for piece in pieces
            ]
            + [
                pl.BlockSpec((block, columns), lambda k, n: (k, 0)),
                pl.BlockSpec(hidden_columns.shape, lambda k, n: (0, 0, 0, 0)),
            ],
            out_specs=[
                pl.BlockSpec((shards, rows, columns), lambda k, n: (0, 0, 0))
                for _ in range(micro_count)
            ],
            scratch_shapes=[pltpu.VMEM((shards * micro_count, rows, columns), jnp.float32)],
        ),
        out_shape=[jax.ShapeDtypeStruct((shards, rows, columns), jnp.bfloat16)] * micro_count,
        name="project",
        compiler_params=pltpu.CompilerParams(vmem_limit_bytes=24 * MIB),
        cost_estimate=pl.CostEstimate(
            flops=2 * shards * micro_count * rows * depth * columns,
            bytes_accessed=2 * depth * columns,
            transcendentals=0,
        ),
    )(me, *pieces, out_weight, hidden_columns)


def experts_kernel(masks, counts, orders, me_ref, *refs):
    pieces, refs = refs[: len(masks)], refs[len(masks) :]
    gain_ref, router_ref, hot_ref, gate_ref, up_ref, down_ref, gu_scale_ref, down_scale_ref = refs[
        :8
    ]
    groups = len(orders)
    send_refs, keep_refs, own_refs = (
        refs[8 + i * groups : 8 + (i + 1) * groups] for i in range(3)
    )
    token_scr, weight_scr, acc_ref = refs[-3:]
    step = pl.program_id(0)
    _, shards, rows, columns = pieces[0].shape
    total, width = token_scr.shape
    part = shards * rows
    me = me_ref[0]

    @pl.when(step == 0)
    def _():
        for m in range(groups):
            mine = [
                (ref, i, mask)
                for ref, mask_list, n in zip(pieces, masks, counts)
                if n == m
                for i, mask in enumerate(mask_list)
            ]
            squares = jnp.zeros((part, columns), jnp.float32)
            for ref, i, _ in mine:
                value = ref[i].reshape(part, columns).astype(jnp.float32)
                squares += value * value
            mean = jnp.sum(squares, axis=-1, keepdims=True) / width
            inverse = lax.rsqrt(mean + 1e-06)
            for ref, i, mask in mine:
                at = pl.ds(0, columns)
                if len(mine) > 1:
                    at = pl.ds(pl.multiple_of((me ^ mask) * columns, columns), columns)
                value = ref[i].reshape(part, columns).astype(jnp.float32)
                own_refs[m][:, at] = ref[i, me]
                token_scr[m * part : (m + 1) * part, at] = (
                    value * inverse * gain_ref[:, at]
                ).astype(jnp.bfloat16)
        logits = lax.dot_general(
            token_scr[...],
            router_ref[...],
            (((1,), (1,)), ((), ())),
            preferred_element_type=jnp.float32,
        )
        hot = hot_ref[...].astype(jnp.float32) > 0.5
        logits = jnp.where(hot, logits, -1e30)
        raised = jnp.where(hot, jnp.exp(logits - jnp.max(logits, axis=-1, keepdims=True)), 0.0)
        raised = raised / jnp.sum(raised, axis=-1, keepdims=True)
        mine = lax.broadcasted_iota(jnp.int32, raised.shape, 1) == me
        weight = jnp.sum(jnp.where(mine, raised, 0.0), axis=-1, keepdims=True)
        weight = weight.astype(jnp.bfloat16).astype(jnp.float32)
        weight_scr[...] = jnp.broadcast_to(weight, (total, LANES)).reshape(weight_scr.shape)
        acc_ref[...] = jnp.zeros_like(acc_ref)

    nt = (((1,), (1,)), ((), ()))
    tokens = token_scr[...]
    gate = lax.dot_general(tokens, gate_ref[...], nt, preferred_element_type=jnp.float32)
    up = lax.dot_general(tokens, up_ref[...], nt, preferred_element_type=jnp.float32)
    gate = gate * gu_scale_ref[0:1, :]
    up = up * gu_scale_ref[1:2, :]
    inner = (gate / (1.0 + jnp.exp(-gate)) * up).astype(jnp.bfloat16)
    piece = 1024
    for c in range(width // piece):
        at = slice(c * piece, (c + 1) * piece)
        product = jnp.dot(inner, down_ref[:, at], preferred_element_type=jnp.float32)
        acc_ref[:, :, at] += product.reshape(groups * shards, rows, piece)

    @pl.when(step == pl.num_programs(0) - 1)
    def _():
        half = shards // 2
        for m, order in enumerate(orders):
            for p, mask in enumerate(order):
                source = m * shards + (me ^ mask)
                value = (acc_ref[source] * down_scale_ref[...]).astype(jnp.bfloat16)
                value = (value.astype(jnp.float32) * weight_scr[source][:, 0:1]).astype(
                    jnp.bfloat16
                )
                if p < half:
                    keep_refs[m][p] = value
                else:
                    send_refs[m][p - half] = value


def run_experts(me, streams, gain, router, hot, gate, up, down, gu_scale, down_scale, orders):
    pieces = [array for chain in streams for array, _ in chain]
    masks = tuple(mask for chain in streams for _, mask in chain)
    counts = tuple(m for m, chain in enumerate(streams) for _ in chain)
    groups = len(streams)
    _, shards, rows, _ = pieces[0].shape
    hidden_units, width = gate.shape
    total = groups * shards * rows
    block = 256
    full = lambda f, n: (0, 0)
    half_spec = pl.BlockSpec((shards // 2, rows, width), lambda f, n: (0, 0, 0))
    half_shape = jax.ShapeDtypeStruct((shards // 2, rows, width), jnp.bfloat16)
    outs = pl.pallas_call(
        functools.partial(experts_kernel, masks, counts, orders),
        grid_spec=pltpu.PrefetchScalarGridSpec(
            num_scalar_prefetch=1,
            grid=(hidden_units // block,),
            in_specs=[pl.BlockSpec(piece.shape, lambda f, n: (0, 0, 0, 0)) for piece in pieces]
            + [
                pl.BlockSpec((1, width), full),
                pl.BlockSpec(router.shape, full),
                pl.BlockSpec(hot.shape, full),
                pl.BlockSpec((block, width), lambda f, n: (f, 0)),
                pl.BlockSpec((block, width), lambda f, n: (f, 0)),
                pl.BlockSpec((block, width), lambda f, n: (f, 0)),
                pl.BlockSpec((2, block), lambda f, n: (0, f)),
                pl.BlockSpec((1, width), full),
            ],
            out_specs=[half_spec] * (2 * groups) + [pl.BlockSpec((rows, width), full)] * groups,
            scratch_shapes=[
                pltpu.VMEM((total, width), jnp.bfloat16),
                pltpu.VMEM((groups * shards, rows, LANES), jnp.float32),
                pltpu.VMEM((groups * shards, rows, width), jnp.float32),
            ],
        ),
        out_shape=[half_shape] * (2 * groups)
        + [jax.ShapeDtypeStruct((rows, width), jnp.bfloat16)] * groups,
        name="experts",
        compiler_params=pltpu.CompilerParams(
            vmem_limit_bytes=(36 if total <= 256 else 60) * MIB
        ),
        cost_estimate=pl.CostEstimate(
            flops=6 * total * width * hidden_units,
            bytes_accessed=6 * width * hidden_units,
            transcendentals=0,
        ),
    )(me, *pieces, gain, router, hot, gate, up, down, gu_scale, down_scale)
    return [tuple(outs[i * groups + m] for i in range(3)) for m in range(groups)]


def swap(value, bit, count):
    return lax.ppermute(value, "expert", [(i, i ^ bit) for i in range(count)])


def gather_all(value, count, near_first):
    if count != 16:
        held, masks = value[None], (0,)
        for bit in [1 << b for b in reversed(range(count.bit_length() - 1))]:
            held = jnp.concatenate([held, swap(held, bit, count)])
            masks = masks + tuple(mask ^ bit for mask in masks)
        return [(held, masks)], []
    if near_first:
        first = jnp.stack([value, swap(value, 2, count)])
        far, near = swap(first, 8, count), swap(first, 4, count)
        both = swap(far, 4, count)
        chain = [(first, (0, 2)), (far, (8, 10)), (near, (4, 6)), (both, (12, 14))]
        marks = [first, far]
    else:
        far, near = swap(value, 8, count), swap(value, 4, count)
        both = swap(far, 4, count)
        first = jnp.stack([value, far, near, both])
        chain = [(first, (0, 8, 4, 12)), (swap(first, 2, count), (2, 10, 6, 14))]
        marks = [far, first]
    chain += [(swap(held, 1, count), tuple(m ^ 1 for m in masks)) for held, masks in chain]
    return chain, marks


def reduce_order(count, flipped):
    bits = [1 << b for b in range(count.bit_length() - 1)]
    if flipped:
        bits = [bits[0]] + bits[2:] + [bits[1]]
    order = tuple(
        sum(bit for i, bit in enumerate(bits) if (p >> (len(bits) - 1 - i)) & 1)
        for p in range(count)
    )
    return bits, order


def reduce_own(send, keep, own, bits, count):
    for i, bit in enumerate(bits):
        other = swap(send, bit, count)
        half = keep.shape[0] // 2
        if half == 0:
            break
        add = lambda a, b: (a.astype(jnp.float32) + b.astype(jnp.float32)).astype(jnp.bfloat16)
        send, keep = add(keep[half:], other[half:]), add(keep[:half], other[:half])
    mixture = keep[0].astype(jnp.float32) + other[0].astype(jnp.float32)
    return (own.astype(jnp.float32) + mixture).astype(jnp.bfloat16)


def body(
    hidden,
    queries,
    kv_cache,
    lengths,
    routes,
    out_weight,
    norm_gain,
    router_weight,
    gate_codes,
    up_codes,
    down_codes,
    codebooks,
    gate_up_scale,
    down_scale,
):
    micro_count, rows, width = hidden.shape
    count = lax.axis_size("expert")
    me = lax.axis_index("expert").astype(jnp.int32)
    me_list = me.reshape(1)
    columns = out_weight.shape[1]
    hot = (routes[..., None] == jnp.arange(count, dtype=jnp.int32)).any(axis=2)
    lead = hidden.reshape(micro_count, rows, count, columns).transpose(2, 0, 1, 3)
    tail = jnp.broadcast_to(hot.astype(jnp.bfloat16)[None], (count,) + hot.shape)
    packed = lax.all_to_all(
        jnp.concatenate([lead, tail], axis=-1), "expert", split_axis=0, concat_axis=0, tiled=True
    )
    hidden_columns = packed[..., :columns]
    hot_all = packed[..., columns:].transpose(1, 0, 2, 3).reshape(micro_count, count * rows, count)

    tables = codebooks[0].astype(jnp.float32).transpose(0, 2, 1).reshape(3, 8, LANES)
    gathered, marks = [], []
    for m in range(micro_count):
        chain, seen = gather_all(attend(queries, kv_cache, lengths, m), count, m % 2 == 1)
        gathered.append(chain)
        marks.append(seen)
    after = [tuple(seen[i] for seen in marks if seen) for i in range(2)]
    gate = expand(tables[0], gate_codes[0].T, True)
    up = expand(tables[1], up_codes[0].T, True, after[0] if marks[0] else ())
    down = expand(tables[2], down_codes[0], False, after[1] if marks[0] else ())

    columns_of = project(me_list, gathered, out_weight, hidden_columns)
    streams = []
    for m in range(micro_count):
        chain, _ = gather_all(columns_of[m], count, m % 2 == 1)
        if columns % LANES:
            held, masks = chain[0]
            place = [masks.index(i) for i in range(count)]
            order = jnp.asarray(place, jnp.int32)[jnp.arange(count, dtype=jnp.int32) ^ me]
            held = held[order].transpose(1, 2, 0, 3).reshape(1, count, rows, width)
            chain = [(held, (0,))]
        streams.append(chain)

    plans = [reduce_order(count, m % 2 == 1) for m in range(micro_count)]
    batches = [list(range(micro_count))] if count * rows <= 128 else [[m] for m in range(micro_count)]
    outputs = []
    for batch in batches:
        results = run_experts(
            me_list,
            [streams[m] for m in batch],
            norm_gain.reshape(1, width),
            router_weight.T,
            jnp.concatenate([hot_all[m] for m in batch]),
            gate,
            up,
            down,
            gate_up_scale[0],
            down_scale,
            tuple(plans[m][1] for m in batch),
        )
        for m, (send, keep, own) in zip(batch, results):
            outputs.append(reduce_own(send, keep, own, plans[m][0], count))
    return jnp.stack(outputs)


def solution(mesh):
    in_specs = (
        P(None, ("groups", "expert"), None),
        P(None, ("groups", "expert"), None),
        P(None, ("groups", "expert"), None, None, None),
        P(None, ("groups", "expert")),
        P(None, ("groups", "expert"), None),
        P(None, "expert"),
        P(),
        P(),
        P("expert", None, None),
        P("expert", None, None),
        P("expert", None, None),
        P("expert", None, None, None),
        P("expert", None, None),
        P("expert", None),
    )
    out_specs = P(None, ("groups", "expert"), None)
    return jax.shard_map(body, mesh=mesh, in_specs=in_specs, out_specs=out_specs, check_vma=False)
```

```python
import functools

import jax
import jax.numpy as jnp
from jax import lax
from jax.experimental import pallas as pl
from jax.experimental.pallas import tpu as pltpu
from jax.sharding import PartitionSpec as P

LANES = 128
KV_HEADS = 4
HEAD_DIM = 128
MIB = 1 << 20


def attend_kernel(micro, span, kv_heads, len_ref, q_ref, kv_ref, out_ref, q_scr, o_scr):
    step = pl.program_id(0)
    rows, width = q_ref.shape
    heads = width // HEAD_DIM
    per_group = heads // kv_heads
    positions = kv_ref.shape[1]

    @pl.when(step == 0)
    def _():
        for h in range(heads):
            q_scr[h] = q_ref[:, h * HEAD_DIM : (h + 1) * HEAD_DIM].astype(jnp.float32)

    column = lax.broadcasted_iota(jnp.int32, (heads, 2 * positions), 1)
    is_key = column % 2 == 0
    blocks, weights = [], []
    for i in range(span):
        row = step * span + i
        parts = [
            kv_ref[i, :, :, g * HEAD_DIM : (g + 1) * HEAD_DIM].reshape(2 * positions, HEAD_DIM)
            for g in range(kv_heads)
        ]
        blocks.append(parts)
        scores = jnp.concatenate(
            [
                lax.dot_general(
                    q_scr[g * per_group : (g + 1) * per_group, row, :].astype(jnp.bfloat16),
                    parts[g],
                    (((1,), (1,)), ((), ())),
                    preferred_element_type=jnp.float32,
                )
                for g in range(kv_heads)
            ],
            axis=0,
        ) * HEAD_DIM ** (-0.5)
        visible = is_key & (column < 2 * len_ref[micro, row])
        scores = jnp.where(visible, scores, -1e30)
        raised = jnp.exp(scores - jnp.max(scores, axis=-1, keepdims=True))
        raised = raised / jnp.sum(raised, axis=-1, keepdims=True)
        weights.append(pltpu.roll(raised, 1, 1).astype(jnp.bfloat16))
    for i in range(span):
        row = step * span + i
        for g in range(kv_heads):
            o_scr[g * per_group : (g + 1) * per_group, row, :] = jnp.dot(
                weights[i][g * per_group : (g + 1) * per_group],
                blocks[i][g],
                preferred_element_type=jnp.float32,
            )

    @pl.when(step == pl.num_programs(0) - 1)
    def _():
        for h in range(heads):
            out_ref[:, h * HEAD_DIM : (h + 1) * HEAD_DIM] = o_scr[h].astype(jnp.bfloat16)


def attend(queries, kv_cache, lengths, micro):
    _, rows, width = queries.shape
    heads = width // HEAD_DIM
    span = 4 if rows % 4 == 0 else 1
    kv_shape = kv_cache.shape[2:]
    return pl.pallas_call(
        functools.partial(attend_kernel, micro, span, KV_HEADS),
        grid_spec=pltpu.PrefetchScalarGridSpec(
            num_scalar_prefetch=1,
            grid=(rows // span,),
            in_specs=[
                pl.BlockSpec((None, rows, width), lambda r, n: (micro, 0, 0)),
                pl.BlockSpec((None, span) + kv_shape, lambda r, n: (micro, r, 0, 0, 0)),
            ],
            out_specs=pl.BlockSpec((rows, width), lambda r, n: (0, 0)),
            scratch_shapes=[pltpu.VMEM((heads, rows, HEAD_DIM), jnp.float32)] * 2,
        ),
        out_shape=jax.ShapeDtypeStruct((rows, width), jnp.bfloat16),
        name="attend",
        compiler_params=pltpu.CompilerParams(vmem_limit_bytes=16 * MIB),
        cost_estimate=pl.CostEstimate(
            flops=rows * width * 4 * 256, bytes_accessed=rows << 18, transcendentals=0
        ),
    )(lengths, queries, pltpu.with_memory_space_constraint(kv_cache, pltpu.HBM))


def expand_kernel(stacked, table_ref, code_ref, *rest):
    out_ref = rest[-1]
    rows, columns = code_ref.shape
    tile = 16
    tables = [jnp.broadcast_to(table_ref[i : i + 1], (tile, LANES)) for i in range(8)]

    def one(i, lane):
        at = pl.ds(pl.multiple_of(i * tile, tile), tile)
        codes = code_ref[at, lane * LANES : (lane + 1) * LANES]
        codes = codes.astype(jnp.float32).astype(jnp.int32)
        upper = codes >= LANES
        low = jnp.bitwise_and(codes, LANES - 1)

        def take(table):
            return jnp.take_along_axis(table, low, axis=1, mode="promise_in_bounds")

        for q in range(4):
            value = jnp.where(upper, take(tables[2 * q + 1]), take(tables[2 * q]))
            value = value.astype(jnp.bfloat16)
            if stacked:
                out_ref[q, at, lane * LANES : (lane + 1) * LANES] = value
            else:
                first = q * columns + lane * LANES
                out_ref[at, first : first + LANES] = value

    for lane in range(columns // LANES):

        def body(i, _, lane=lane):
            one(i, lane)
            return 0

        lax.fori_loop(0, rows // tile, body, 0, unroll=rows // tile if rows // tile <= 12 else 8)


def expand(table, codes, stacked, after=()):
    rows, columns = codes.shape
    if stacked:
        block = 512
        grid = (columns // block,)
        code_spec = pl.BlockSpec((rows, block), lambda b: (0, b))
        out_spec = pl.BlockSpec((4, rows, block), lambda b: (0, 0, b))
        out_shape = (4, rows, columns)
    else:
        block = 128
        grid = (rows // block,)
        code_spec = pl.BlockSpec((block, columns), lambda b: (b, 0))
        out_spec = pl.BlockSpec((block, 4 * columns), lambda b: (b, 0))
        out_shape = (rows, 4 * columns)
    out = pl.pallas_call(
        functools.partial(expand_kernel, stacked),
        grid=grid,
        in_specs=[pl.BlockSpec((8, LANES), lambda b: (0, 0)), code_spec]
        + [pl.BlockSpec(memory_space=pl.ANY) for _ in after],
        out_specs=out_spec,
        out_shape=jax.ShapeDtypeStruct(out_shape, jnp.bfloat16),
        name="expand",
        compiler_params=pltpu.CompilerParams(vmem_limit_bytes=10 * MIB),
        cost_estimate=pl.CostEstimate(
            flops=rows * columns * 8000, bytes_accessed=10 * rows * columns, transcendentals=0
        ),
    )(table, pltpu.with_memory_space_constraint(codes, pltpu.HBM), *after)
    return out.reshape(4 * rows, columns) if stacked else out


def project_kernel(masks, counts, me_ref, *refs):
    pieces, refs = refs[: len(masks)], refs[len(masks) :]
    weight_ref, hidden_ref = refs[:2]
    out_refs, acc_ref = refs[2:-1], refs[-1]
    step = pl.program_id(0)
    depth = weight_ref.shape[0]

    @pl.when(step == 0)
    def _():
        acc_ref[...] = jnp.zeros_like(acc_ref)

    rows_in = jnp.concatenate([ref[...].reshape(-1, depth) for ref in pieces], axis=0)
    product = jnp.dot(rows_in, weight_ref[...], preferred_element_type=jnp.float32)
    acc_ref[...] += product.reshape(acc_ref.shape)

    @pl.when(step == pl.num_programs(0) - 1)
    def _():
        me = me_ref[0]
        at = 0
        for mask_list, m in zip(masks, counts):
            for mask in mask_list:
                source = me ^ mask
                projected = acc_ref[at].astype(jnp.bfloat16).astype(jnp.float32)
                out_refs[m][source] = (
                    hidden_ref[source, m].astype(jnp.float32) + projected
                ).astype(jnp.bfloat16)
                at += 1


def project(me, gathered, out_weight, hidden_columns):
    pieces = [array for chain in gathered for array, _ in chain]
    masks = tuple(mask for chain in gathered for _, mask in chain)
    counts = tuple(m for m, chain in enumerate(gathered) for _ in chain)
    shards, micro_count, rows, columns = hidden_columns.shape
    depth = out_weight.shape[0]
    block = 2048
    return pl.pallas_call(
        functools.partial(project_kernel, masks, counts),
        grid_spec=pltpu.PrefetchScalarGridSpec(
            num_scalar_prefetch=1,
            grid=(depth // block,),
            in_specs=[
                pl.BlockSpec((piece.shape[0], rows, block), lambda k, n: (0, 0, k))
                for piece in pieces
            ]
            + [
                pl.BlockSpec((block, columns), lambda k, n: (k, 0)),
                pl.BlockSpec(hidden_columns.shape, lambda k, n: (0, 0, 0, 0)),
            ],
            out_specs=[
                pl.BlockSpec((shards, rows, columns), lambda k, n: (0, 0, 0))
                for _ in range(micro_count)
            ],
            scratch_shapes=[pltpu.VMEM((shards * micro_count, rows, columns), jnp.float32)],
        ),
        out_shape=[jax.ShapeDtypeStruct((shards, rows, columns), jnp.bfloat16)] * micro_count,
        name="project",
        compiler_params=pltpu.CompilerParams(vmem_limit_bytes=24 * MIB),
        cost_estimate=pl.CostEstimate(
            flops=2 * shards * micro_count * rows * depth * columns,
            bytes_accessed=2 * depth * columns,
            transcendentals=0,
        ),
    )(me, *pieces, pltpu.with_memory_space_constraint(out_weight, pltpu.HBM), hidden_columns)


def experts_kernel(masks, counts, orders, me_ref, *refs):
    pieces, refs = refs[: len(masks)], refs[len(masks) :]
    gain_ref, router_ref, hot_ref, gate_ref, up_ref, down_ref, gu_scale_ref, down_scale_ref = refs[
        :8
    ]
    groups = len(orders)
    send_refs, keep_refs, own_refs = (
        refs[8 + i * groups : 8 + (i + 1) * groups] for i in range(3)
    )
    token_scr, weight_scr, acc_ref = refs[-3:]
    _, shards, rows, columns = pieces[0].shape
    total, width = token_scr.shape
    part = shards * rows
    hidden_units = gate_ref.shape[0]
    me = me_ref[0]
    nt = (((1,), (1,)), ((), ()))

    for m in range(groups):
        mine = [
            (ref, i, mask)
            for ref, mask_list, n in zip(pieces, masks, counts)
            if n == m
            for i, mask in enumerate(mask_list)
        ]
        squares = jnp.zeros((part, columns), jnp.float32)
        for ref, i, _ in mine:
            value = ref[i].reshape(part, columns).astype(jnp.float32)
            squares += value * value
        mean = jnp.sum(squares, axis=-1, keepdims=True) / width
        inverse = lax.rsqrt(mean + 1e-06)
        for ref, i, mask in mine:
            at = pl.ds(0, columns)
            if len(mine) > 1:
                at = pl.ds(pl.multiple_of((me ^ mask) * columns, columns), columns)
            value = ref[i].reshape(part, columns).astype(jnp.float32)
            own_refs[m][:, at] = ref[i, me]
            token_scr[m * part : (m + 1) * part, at] = (
                value * inverse * gain_ref[:, at]
            ).astype(jnp.bfloat16)
    logits = lax.dot_general(
        token_scr[...], router_ref[...], nt, preferred_element_type=jnp.float32
    )
    hot = hot_ref[...].astype(jnp.float32) > 0.5
    logits = jnp.where(hot, logits, -1e30)
    raised = jnp.where(hot, jnp.exp(logits - jnp.max(logits, axis=-1, keepdims=True)), 0.0)
    raised = raised / jnp.sum(raised, axis=-1, keepdims=True)
    column = lax.broadcasted_iota(jnp.int32, raised.shape, 1) == me
    weight = jnp.sum(jnp.where(column, raised, 0.0), axis=-1, keepdims=True)
    weight = weight.astype(jnp.bfloat16).astype(jnp.float32)
    weight_scr[...] = jnp.broadcast_to(weight, (total, LANES)).reshape(weight_scr.shape)

    block, piece = 256, 1024
    for f in range(hidden_units // block):
        units = slice(f * block, (f + 1) * block)
        tokens = token_scr[...]
        gate = lax.dot_general(tokens, gate_ref[units, :], nt, preferred_element_type=jnp.float32)
        up = lax.dot_general(tokens, up_ref[units, :], nt, preferred_element_type=jnp.float32)
        gate = gate * gu_scale_ref[0:1, units]
        up = up * gu_scale_ref[1:2, units]
        inner = (gate / (1.0 + jnp.exp(-gate)) * up).astype(jnp.bfloat16)
        for c in range(width // piece):
            at = slice(c * piece, (c + 1) * piece)
            product = jnp.dot(inner, down_ref[units, at], preferred_element_type=jnp.float32)
            product = product.reshape(groups * shards, rows, piece)
            if f == 0:
                acc_ref[:, :, at] = product
            else:
                acc_ref[:, :, at] += product

    half = shards // 2
    for m, order in enumerate(orders):
        for p, mask in enumerate(order):
            source = m * shards + (me ^ mask)
            value = (acc_ref[source] * down_scale_ref[...]).astype(jnp.bfloat16)
            value = (value.astype(jnp.float32) * weight_scr[source][:, 0:1]).astype(jnp.bfloat16)
            if p < half:
                keep_refs[m][p] = value
            else:
                send_refs[m][p - half] = value


def run_experts(me, streams, gain, router, hot, gate, up, down, gu_scale, down_scale, orders):
    pieces = [array for chain in streams for array, _ in chain]
    masks = tuple(mask for chain in streams for _, mask in chain)
    counts = tuple(m for m, chain in enumerate(streams) for _ in chain)
    groups = len(streams)
    _, shards, rows, _ = pieces[0].shape
    hidden_units, width = gate.shape
    total = groups * shards * rows
    half_shape = jax.ShapeDtypeStruct((shards // 2, rows, width), jnp.bfloat16)
    in_vmem = pl.BlockSpec(memory_space=pltpu.VMEM)
    held = [gate, up, down]
    if total <= 256:
        held = [pltpu.with_memory_space_constraint(w, pltpu.VMEM) for w in held]
        pieces = [pltpu.with_memory_space_constraint(w, pltpu.VMEM) for w in pieces]
    outs = pl.pallas_call(
        functools.partial(experts_kernel, masks, counts, orders),
        in_specs=[pl.BlockSpec(memory_space=pltpu.SMEM)] + [in_vmem] * (len(pieces) + 8),
        out_specs=[in_vmem] * (3 * groups),
        out_shape=[half_shape] * (2 * groups)
        + [jax.ShapeDtypeStruct((rows, width), jnp.bfloat16)] * groups,
        scratch_shapes=[
            pltpu.VMEM((total, width), jnp.bfloat16),
            pltpu.VMEM((groups * shards, rows, LANES), jnp.float32),
            pltpu.VMEM((groups * shards, rows, width), jnp.float32),
        ],
        name="experts",
        compiler_params=pltpu.CompilerParams(vmem_limit_bytes=(24 if total <= 256 else 62) * MIB),
        cost_estimate=pl.CostEstimate(
            flops=6 * total * width * hidden_units,
            bytes_accessed=6 * width * hidden_units,
            transcendentals=0,
        ),
    )(me, *pieces, gain, router, hot, *held, gu_scale, down_scale)
    return [tuple(outs[i * groups + m] for i in range(3)) for m in range(groups)]


def swap(value, bit, count):
    return lax.ppermute(value, "expert", [(i, i ^ bit) for i in range(count)])


def tie(value, *earlier):
    return lax.optimization_barrier((value,) + earlier)[0]


def gather_all(value, count):
    held, masks = value[None], (0,)
    for bit in [1 << b for b in reversed(range(count.bit_length() - 1))]:
        held = jnp.concatenate([held, swap(held, bit, count)])
        masks = masks + tuple(mask ^ bit for mask in masks)
    return [(held, masks)]


def gather_two(one, two, fillers):
    count = 16
    far_one, near_one = swap(one, 8, count), swap(one, 4, count)
    pair_two = jnp.stack([two, swap(two, 2, count)])
    far_two, near_two = swap(pair_two, 8, count), swap(pair_two, 4, count)
    both_one = swap(far_one, 4, count)
    four_one = jnp.stack([one, far_one, near_one, both_one])
    side_one = swap(four_one, 2, count)
    done = [fillers[0]((four_one, pair_two))]
    both_two = swap(tie(far_two, done[0]), 4, count)
    if len(fillers) > 1:
        done.append(fillers[1]((far_two, done[0])))
    chain_one = [(four_one, (0, 8, 4, 12)), (side_one, (2, 10, 6, 14))]
    chain_two = [(pair_two, (0, 2)), (far_two, (8, 10)), (near_two, (4, 6)), (both_two, (12, 14))]
    for chain in (chain_one, chain_two):
        for i, (held, masks) in enumerate(list(chain)):
            if i:
                held = tie(held, done[-1])
            chain.append((swap(held, 1, count), tuple(m ^ 1 for m in masks)))
    return [chain_one, chain_two], done


def reduce_order(count, flipped):
    bits = [1 << b for b in range(count.bit_length() - 1)]
    if flipped:
        bits = [bits[0]] + bits[2:] + [bits[1]]
    order = tuple(
        sum(bit for i, bit in enumerate(bits) if (p >> (len(bits) - 1 - i)) & 1)
        for p in range(count)
    )
    return bits, order


def reduce_own(send, keep, own, bits, count):
    for i, bit in enumerate(bits):
        other = swap(send, bit, count)
        half = keep.shape[0] // 2
        if half == 0:
            break
        add = lambda a, b: (a.astype(jnp.float32) + b.astype(jnp.float32)).astype(jnp.bfloat16)
        send, keep = add(keep[half:], other[half:]), add(keep[:half], other[:half])
    mixture = keep[0].astype(jnp.float32) + other[0].astype(jnp.float32)
    return (own.astype(jnp.float32) + mixture).astype(jnp.bfloat16)


def body(
    hidden,
    queries,
    kv_cache,
    lengths,
    routes,
    out_weight,
    norm_gain,
    router_weight,
    gate_codes,
    up_codes,
    down_codes,
    codebooks,
    gate_up_scale,
    down_scale,
):
    micro_count, rows, width = hidden.shape
    count = lax.axis_size("expert")
    me = lax.axis_index("expert").astype(jnp.int32)
    me_list = me.reshape(1)
    columns = out_weight.shape[1]
    hot = (routes[..., None] == jnp.arange(count, dtype=jnp.int32)).any(axis=2)
    lead = hidden.reshape(micro_count, rows, count, columns).transpose(2, 0, 1, 3)
    tail = jnp.broadcast_to(hot.astype(jnp.bfloat16)[None], (count,) + hot.shape)
    packed = lax.all_to_all(
        jnp.concatenate([lead, tail], axis=-1), "expert", split_axis=0, concat_axis=0, tiled=True
    )
    hidden_columns = packed[..., :columns]
    hot_all = packed[..., columns:].transpose(1, 0, 2, 3).reshape(micro_count, count * rows, count)

    tables = codebooks[0].astype(jnp.float32).transpose(0, 2, 1).reshape(3, 8, LANES)
    attended = [attend(queries, kv_cache, lengths, m) for m in range(micro_count)]
    make_gate = lambda after: expand(tables[0], gate_codes[0].T, True, after)
    make_up = lambda after: expand(tables[1], up_codes[0].T, True, after + (packed,))
    make_down = lambda after: expand(tables[2], down_codes[0], False, after)
    if count == 16 and micro_count == 2:
        gathered, (gate, up) = gather_two(*attended, [make_gate, make_up])
        column_parts = project(me_list, gathered, out_weight, hidden_columns)
        streams, (down,) = gather_two(*column_parts, [make_down])
    else:
        gate, up, down = make_gate(()), make_up(()), make_down(())
        gathered = [gather_all(value, count) for value in attended]
        column_parts = project(me_list, gathered, out_weight, hidden_columns)
        streams = [gather_all(value, count) for value in column_parts]
    if columns % LANES:
        joined = []
        for ((held, masks),) in streams:
            place = jnp.asarray([masks.index(i) for i in range(count)], jnp.int32)
            held = held[place[jnp.arange(count, dtype=jnp.int32) ^ me]]
            held = held.transpose(1, 2, 0, 3).reshape(1, count, rows, width)
            joined.append([(held, (0,))])
        streams = joined

    plans = [reduce_order(count, m % 2 == 1) for m in range(micro_count)]
    batches = [list(range(micro_count))] if count * rows <= 128 else [[m] for m in range(micro_count)]
    outputs = []
    for batch in batches:
        results = run_experts(
            me_list,
            [streams[m] for m in batch],
            norm_gain.reshape(1, width),
            router_weight.T,
            jnp.concatenate([hot_all[m] for m in batch]),
            gate,
            up,
            down,
            gate_up_scale[0],
            down_scale,
            tuple(plans[m][1] for m in batch),
        )
        for m, (send, keep, own) in zip(batch, results):
            outputs.append(reduce_own(send, keep, own, plans[m][0], count))
    return jnp.stack(outputs)


def solution(mesh):
    in_specs = (
        P(None, ("groups", "expert"), None),
        P(None, ("groups", "expert"), None),
        P(None, ("groups", "expert"), None, None, None),
        P(None, ("groups", "expert")),
        P(None, ("groups", "expert"), None),
        P(None, "expert"),
        P(),
        P(),
        P("expert", None, None),
        P("expert", None, None),
        P("expert", None, None),
        P("expert", None, None, None),
        P("expert", None, None),
        P("expert", None),
    )
    out_specs = P(None, ("groups", "expert"), None)
    return jax.shard_map(body, mesh=mesh, in_specs=in_specs, out_specs=out_specs, check_vma=False)
```

```python
import functools

import jax
import jax.numpy as jnp
from jax import lax
from jax.experimental import pallas as pl
from jax.experimental.pallas import tpu as pltpu
from jax.sharding import PartitionSpec as P

LANES = 128
KV_HEADS = 4
HEAD_DIM = 128
MIB = 1 << 20


def attend_kernel(micro, span, kv_heads, len_ref, q_ref, kv_ref, out_ref, q_scr, o_scr):
    step = pl.program_id(0)
    rows, width = q_ref.shape
    heads = width // HEAD_DIM
    per_group = heads // kv_heads
    positions = kv_ref.shape[1]

    @pl.when(step == 0)
    def _():
        for h in range(heads):
            q_scr[h] = q_ref[:, h * HEAD_DIM : (h + 1) * HEAD_DIM].astype(jnp.float32)

    column = lax.broadcasted_iota(jnp.int32, (heads, 2 * positions), 1)
    is_key = column % 2 == 0
    blocks, weights = [], []
    for i in range(span):
        row = step * span + i
        parts = [
            kv_ref[i, :, :, g * HEAD_DIM : (g + 1) * HEAD_DIM].reshape(2 * positions, HEAD_DIM)
            for g in range(kv_heads)
        ]
        blocks.append(parts)
        scores = jnp.concatenate(
            [
                lax.dot_general(
                    q_scr[g * per_group : (g + 1) * per_group, row, :].astype(jnp.bfloat16),
                    parts[g],
                    (((1,), (1,)), ((), ())),
                    preferred_element_type=jnp.float32,
                )
                for g in range(kv_heads)
            ],
            axis=0,
        ) * HEAD_DIM ** (-0.5)
        visible = is_key & (column < 2 * len_ref[micro, row])
        scores = jnp.where(visible, scores, -1e30)
        raised = jnp.exp(scores - jnp.max(scores, axis=-1, keepdims=True))
        raised = raised / jnp.sum(raised, axis=-1, keepdims=True)
        weights.append(pltpu.roll(raised, 1, 1).astype(jnp.bfloat16))
    for i in range(span):
        row = step * span + i
        for g in range(kv_heads):
            o_scr[g * per_group : (g + 1) * per_group, row, :] = jnp.dot(
                weights[i][g * per_group : (g + 1) * per_group],
                blocks[i][g],
                preferred_element_type=jnp.float32,
            )

    @pl.when(step == pl.num_programs(0) - 1)
    def _():
        for h in range(heads):
            out_ref[:, h * HEAD_DIM : (h + 1) * HEAD_DIM] = o_scr[h].astype(jnp.bfloat16)


def attend(queries, kv_cache, lengths, micro):
    _, rows, width = queries.shape
    heads = width // HEAD_DIM
    span = 4 if rows % 4 == 0 else 1
    kv_shape = kv_cache.shape[2:]
    return pl.pallas_call(
        functools.partial(attend_kernel, micro, span, KV_HEADS),
        grid_spec=pltpu.PrefetchScalarGridSpec(
            num_scalar_prefetch=1,
            grid=(rows // span,),
            in_specs=[
                pl.BlockSpec((None, rows, width), lambda r, n: (micro, 0, 0)),
                pl.BlockSpec((None, span) + kv_shape, lambda r, n: (micro, r, 0, 0, 0)),
            ],
            out_specs=pl.BlockSpec((rows, width), lambda r, n: (0, 0)),
            scratch_shapes=[pltpu.VMEM((heads, rows, HEAD_DIM), jnp.float32)] * 2,
        ),
        out_shape=jax.ShapeDtypeStruct((rows, width), jnp.bfloat16),
        name="attend",
        compiler_params=pltpu.CompilerParams(vmem_limit_bytes=16 * MIB),
        cost_estimate=pl.CostEstimate(
            flops=rows * width * 4 * 256, bytes_accessed=rows << 18, transcendentals=0
        ),
    )(lengths, queries, pltpu.with_memory_space_constraint(kv_cache, pltpu.HBM))


def expand_kernel(stacked, table_ref, code_ref, out_ref):
    rows, columns = code_ref.shape
    tile = 16
    tables = [jnp.broadcast_to(table_ref[i : i + 1], (tile, LANES)) for i in range(8)]

    def one(i, lane):
        at = pl.ds(pl.multiple_of(i * tile, tile), tile)
        codes = code_ref[at, lane * LANES : (lane + 1) * LANES]
        codes = codes.astype(jnp.float32).astype(jnp.int32)
        upper = codes >= LANES
        low = jnp.bitwise_and(codes, LANES - 1)

        def take(table):
            return jnp.take_along_axis(table, low, axis=1, mode="promise_in_bounds")

        for q in range(4):
            value = jnp.where(upper, take(tables[2 * q + 1]), take(tables[2 * q]))
            value = value.astype(jnp.bfloat16)
            if stacked:
                out_ref[q, at, lane * LANES : (lane + 1) * LANES] = value
            else:
                first = q * columns + lane * LANES
                out_ref[at, first : first + LANES] = value

    for lane in range(columns // LANES):

        def body(i, _, lane=lane):
            one(i, lane)
            return 0

        lax.fori_loop(0, rows // tile, body, 0, unroll=rows // tile if rows // tile <= 12 else 8)


def expand(table, codes, stacked, after=()):
    rows, columns = codes.shape
    if stacked:
        block = 512
        grid = (columns // block,)
        code_spec = pl.BlockSpec((rows, block), lambda b: (0, b))
        out_spec = pl.BlockSpec((4, rows, block), lambda b: (0, 0, b))
        out_shape = (4, rows, columns)
    else:
        block = 128
        grid = (rows // block,)
        code_spec = pl.BlockSpec((block, columns), lambda b: (b, 0))
        out_spec = pl.BlockSpec((block, 4 * columns), lambda b: (b, 0))
        out_shape = (rows, 4 * columns)
    out = pl.pallas_call(
        functools.partial(expand_kernel, stacked),
        grid=grid,
        in_specs=[pl.BlockSpec((8, LANES), lambda b: (0, 0)), code_spec],
        out_specs=out_spec,
        out_shape=jax.ShapeDtypeStruct(out_shape, jnp.bfloat16),
        name="expand",
        compiler_params=pltpu.CompilerParams(vmem_limit_bytes=10 * MIB),
        cost_estimate=pl.CostEstimate(
            flops=rows * columns * 8000, bytes_accessed=10 * rows * columns, transcendentals=0
        ),
    )(tie(table, *after), pltpu.with_memory_space_constraint(codes, pltpu.HBM))
    return out.reshape(4 * rows, columns) if stacked else out


def project_kernel(masks, counts, me_ref, *refs):
    pieces, refs = refs[: len(masks)], refs[len(masks) :]
    weight_ref, hidden_ref = refs[:2]
    out_refs, acc_ref = refs[2:-1], refs[-1]
    step = pl.program_id(0)
    depth = weight_ref.shape[0]

    @pl.when(step == 0)
    def _():
        acc_ref[...] = jnp.zeros_like(acc_ref)

    rows_in = jnp.concatenate([ref[...].reshape(-1, depth) for ref in pieces], axis=0)
    product = jnp.dot(rows_in, weight_ref[...], preferred_element_type=jnp.float32)
    acc_ref[...] += product.reshape(acc_ref.shape)

    @pl.when(step == pl.num_programs(0) - 1)
    def _():
        me = me_ref[0]
        at = 0
        for mask_list, m in zip(masks, counts):
            for mask in mask_list:
                source = me ^ mask
                projected = acc_ref[at].astype(jnp.bfloat16).astype(jnp.float32)
                out_refs[m][source] = (
                    hidden_ref[source, m].astype(jnp.float32) + projected
                ).astype(jnp.bfloat16)
                at += 1


def project(me, gathered, out_weight, hidden_columns):
    pieces = [array for chain in gathered for array, _ in chain]
    masks = tuple(mask for chain in gathered for _, mask in chain)
    counts = tuple(m for m, chain in enumerate(gathered) for _ in chain)
    shards, micro_count, rows, columns = hidden_columns.shape
    depth = out_weight.shape[0]
    block = 2048
    return pl.pallas_call(
        functools.partial(project_kernel, masks, counts),
        grid_spec=pltpu.PrefetchScalarGridSpec(
            num_scalar_prefetch=1,
            grid=(depth // block,),
            in_specs=[
                pl.BlockSpec((piece.shape[0], rows, block), lambda k, n: (0, 0, k))
                for piece in pieces
            ]
            + [
                pl.BlockSpec((block, columns), lambda k, n: (k, 0)),
                pl.BlockSpec(hidden_columns.shape, lambda k, n: (0, 0, 0, 0)),
            ],
            out_specs=[
                pl.BlockSpec((shards, rows, columns), lambda k, n: (0, 0, 0))
                for _ in range(micro_count)
            ],
            scratch_shapes=[pltpu.VMEM((shards * micro_count, rows, columns), jnp.float32)],
        ),
        out_shape=[jax.ShapeDtypeStruct((shards, rows, columns), jnp.bfloat16)] * micro_count,
        name="project",
        compiler_params=pltpu.CompilerParams(vmem_limit_bytes=24 * MIB),
        cost_estimate=pl.CostEstimate(
            flops=2 * shards * micro_count * rows * depth * columns,
            bytes_accessed=2 * depth * columns,
            transcendentals=0,
        ),
    )(me, *pieces, pltpu.with_memory_space_constraint(out_weight, pltpu.HBM), hidden_columns)


def experts_kernel(masks, counts, orders, me_ref, *refs):
    pieces, refs = refs[: len(masks)], refs[len(masks) :]
    gain_ref, router_ref, hot_ref, gate_ref, up_ref, down_ref, gu_scale_ref, down_scale_ref = refs[
        :8
    ]
    groups = len(orders)
    send_refs, keep_refs, own_refs = (
        refs[8 + i * groups : 8 + (i + 1) * groups] for i in range(3)
    )
    token_scr, weight_scr, acc_ref = refs[-3:]
    _, shards, rows, columns = pieces[0].shape
    total, width = token_scr.shape
    part = shards * rows
    hidden_units = gate_ref.shape[0]
    me = me_ref[0]
    nt = (((1,), (1,)), ((), ()))

    for m in range(groups):
        mine = [
            (ref, i, mask)
            for ref, mask_list, n in zip(pieces, masks, counts)
            if n == m
            for i, mask in enumerate(mask_list)
        ]
        squares = jnp.zeros((part, columns), jnp.float32)
        for ref, i, _ in mine:
            value = ref[i].reshape(part, columns).astype(jnp.float32)
            squares += value * value
        mean = jnp.sum(squares, axis=-1, keepdims=True) / width
        inverse = lax.rsqrt(mean + 1e-06)
        for ref, i, mask in mine:
            at = pl.ds(0, columns)
            if len(mine) > 1:
                at = pl.ds(pl.multiple_of((me ^ mask) * columns, columns), columns)
            value = ref[i].reshape(part, columns).astype(jnp.float32)
            own_refs[m][:, at] = ref[i, me]
            token_scr[m * part : (m + 1) * part, at] = (
                value * inverse * gain_ref[:, at]
            ).astype(jnp.bfloat16)
    logits = lax.dot_general(
        token_scr[...], router_ref[...], nt, preferred_element_type=jnp.float32
    )
    hot = hot_ref[...].astype(jnp.float32) > 0.5
    logits = jnp.where(hot, logits, -1e30)
    raised = jnp.where(hot, jnp.exp(logits - jnp.max(logits, axis=-1, keepdims=True)), 0.0)
    raised = raised / jnp.sum(raised, axis=-1, keepdims=True)
    column = lax.broadcasted_iota(jnp.int32, raised.shape, 1) == me
    weight = jnp.sum(jnp.where(column, raised, 0.0), axis=-1, keepdims=True)
    weight = weight.astype(jnp.bfloat16).astype(jnp.float32)
    weight_scr[...] = jnp.broadcast_to(weight, (total, LANES)).reshape(weight_scr.shape)

    block, piece = 256, 1024
    for f in range(hidden_units // block):
        units = slice(f * block, (f + 1) * block)
        tokens = token_scr[...]
        gate = lax.dot_general(tokens, gate_ref[units, :], nt, preferred_element_type=jnp.float32)
        up = lax.dot_general(tokens, up_ref[units, :], nt, preferred_element_type=jnp.float32)
        gate = gate * gu_scale_ref[0:1, units]
        up = up * gu_scale_ref[1:2, units]
        inner = (gate / (1.0 + jnp.exp(-gate)) * up).astype(jnp.bfloat16)
        for c in range(width // piece):
            at = slice(c * piece, (c + 1) * piece)
            product = jnp.dot(inner, down_ref[units, at], preferred_element_type=jnp.float32)
            product = product.reshape(groups * shards, rows, piece)
            if f == 0:
                acc_ref[:, :, at] = product
            else:
                acc_ref[:, :, at] += product

    half = shards // 2
    for m, order in enumerate(orders):
        for p, mask in enumerate(order):
            source = m * shards + (me ^ mask)
            value = (acc_ref[source] * down_scale_ref[...]).astype(jnp.bfloat16)
            value = (value.astype(jnp.float32) * weight_scr[source][:, 0:1]).astype(jnp.bfloat16)
            if p < half:
                keep_refs[m][p] = value
            else:
                send_refs[m][p - half] = value


def run_experts(me, streams, gain, router, hot, gate, up, down, gu_scale, down_scale, orders):
    pieces = [array for chain in streams for array, _ in chain]
    masks = tuple(mask for chain in streams for _, mask in chain)
    counts = tuple(m for m, chain in enumerate(streams) for _ in chain)
    groups = len(streams)
    _, shards, rows, _ = pieces[0].shape
    hidden_units, width = gate.shape
    total = groups * shards * rows
    half_shape = jax.ShapeDtypeStruct((shards // 2, rows, width), jnp.bfloat16)
    in_vmem = pl.BlockSpec(memory_space=pltpu.VMEM)
    held = [gate, up, down]
    if total <= 256:
        held = [pltpu.with_memory_space_constraint(w, pltpu.VMEM) for w in held]
        pieces = [pltpu.with_memory_space_constraint(w, pltpu.VMEM) for w in pieces]
    outs = pl.pallas_call(
        functools.partial(experts_kernel, masks, counts, orders),
        in_specs=[pl.BlockSpec(memory_space=pltpu.SMEM)] + [in_vmem] * (len(pieces) + 8),
        out_specs=[in_vmem] * (3 * groups),
        out_shape=[half_shape] * (2 * groups)
        + [jax.ShapeDtypeStruct((rows, width), jnp.bfloat16)] * groups,
        scratch_shapes=[
            pltpu.VMEM((total, width), jnp.bfloat16),
            pltpu.VMEM((groups * shards, rows, LANES), jnp.float32),
            pltpu.VMEM((groups * shards, rows, width), jnp.float32),
        ],
        name="experts",
        compiler_params=pltpu.CompilerParams(vmem_limit_bytes=(24 if total <= 256 else 62) * MIB),
        cost_estimate=pl.CostEstimate(
            flops=6 * total * width * hidden_units,
            bytes_accessed=6 * width * hidden_units,
            transcendentals=0,
        ),
    )(me, *pieces, gain, router, hot, *held, gu_scale, down_scale)
    return [tuple(outs[i * groups + m] for i in range(3)) for m in range(groups)]


def swap(value, bit, count):
    return lax.ppermute(value, "expert", [(i, i ^ bit) for i in range(count)])


def tie(value, *earlier):
    return lax.optimization_barrier((value,) + earlier)[0]


def gather_all(value, count):
    held, masks = value[None], (0,)
    for bit in [1 << b for b in reversed(range(count.bit_length() - 1))]:
        held = jnp.concatenate([held, swap(held, bit, count)])
        masks = masks + tuple(mask ^ bit for mask in masks)
    return [(held, masks)]


def gather_two(one, two, fillers):
    count = 16
    far_one, near_one = swap(one, 8, count), swap(one, 4, count)
    pair_two = jnp.stack([two, swap(two, 2, count)])
    far_two, near_two = swap(pair_two, 8, count), swap(pair_two, 4, count)
    both_one = swap(far_one, 4, count)
    four_one = jnp.stack([one, far_one, near_one, both_one])
    side_one = swap(four_one, 2, count)
    done = [fillers[0]((four_one, pair_two))]
    both_two = swap(tie(far_two, done[0]), 4, count)
    if len(fillers) > 1:
        done.append(fillers[1]((far_two, done[0])))
    chain_one = [(four_one, (0, 8, 4, 12)), (side_one, (2, 10, 6, 14))]
    chain_two = [(pair_two, (0, 2)), (far_two, (8, 10)), (near_two, (4, 6)), (both_two, (12, 14))]
    for chain in (chain_one, chain_two):
        for i, (held, masks) in enumerate(list(chain)):
            if i:
                held = tie(held, done[-1])
            chain.append((swap(held, 1, count), tuple(m ^ 1 for m in masks)))
    return [chain_one, chain_two], done


def reduce_order(count, flipped):
    bits = [1 << b for b in range(count.bit_length() - 1)]
    if flipped:
        bits = [bits[0]] + bits[2:] + [bits[1]]
    order = tuple(
        sum(bit for i, bit in enumerate(bits) if (p >> (len(bits) - 1 - i)) & 1)
        for p in range(count)
    )
    return bits, order


def reduce_own(send, keep, own, bits, count):
    for i, bit in enumerate(bits):
        other = swap(send, bit, count)
        half = keep.shape[0] // 2
        if half == 0:
            break
        add = lambda a, b: (a.astype(jnp.float32) + b.astype(jnp.float32)).astype(jnp.bfloat16)
        send, keep = add(keep[half:], other[half:]), add(keep[:half], other[:half])
    mixture = keep[0].astype(jnp.float32) + other[0].astype(jnp.float32)
    return (own.astype(jnp.float32) + mixture).astype(jnp.bfloat16)


def body(
    hidden,
    queries,
    kv_cache,
    lengths,
    routes,
    out_weight,
    norm_gain,
    router_weight,
    gate_codes,
    up_codes,
    down_codes,
    codebooks,
    gate_up_scale,
    down_scale,
):
    micro_count, rows, width = hidden.shape
    count = lax.axis_size("expert")
    me = lax.axis_index("expert").astype(jnp.int32)
    me_list = me.reshape(1)
    columns = out_weight.shape[1]
    hot = (routes[..., None] == jnp.arange(count, dtype=jnp.int32)).any(axis=2)
    lead = hidden.reshape(micro_count, rows, count, columns).transpose(2, 0, 1, 3)
    tail = jnp.broadcast_to(hot.astype(jnp.bfloat16)[None], (count,) + hot.shape)
    packed = lax.all_to_all(
        jnp.concatenate([lead, tail], axis=-1), "expert", split_axis=0, concat_axis=0, tiled=True
    )
    hidden_columns = packed[..., :columns]
    hot_all = packed[..., columns:].transpose(1, 0, 2, 3).reshape(micro_count, count * rows, count)

    tables = codebooks[0].astype(jnp.float32).transpose(0, 2, 1).reshape(3, 8, LANES)
    attended = [attend(queries, kv_cache, lengths, m) for m in range(micro_count)]
    make_gate = lambda after: expand(tables[0], gate_codes[0].T, True, after)
    make_up = lambda after: expand(tables[1], up_codes[0].T, True, after + (packed,))
    make_down = lambda after: expand(tables[2], down_codes[0], False, after)
    if count == 16 and micro_count == 2:
        gathered, (gate, up) = gather_two(*attended, [make_gate, make_up])
        column_parts = project(me_list, gathered, out_weight, hidden_columns)
        streams, (down,) = gather_two(*column_parts, [make_down])
    else:
        gate, up, down = make_gate(()), make_up(()), make_down(())
        gathered = [gather_all(value, count) for value in attended]
        column_parts = project(me_list, gathered, out_weight, hidden_columns)
        streams = [gather_all(value, count) for value in column_parts]
    if columns % LANES:
        joined = []
        for ((held, masks),) in streams:
            place = jnp.asarray([masks.index(i) for i in range(count)], jnp.int32)
            held = held[place[jnp.arange(count, dtype=jnp.int32) ^ me]]
            held = held.transpose(1, 2, 0, 3).reshape(1, count, rows, width)
            joined.append([(held, (0,))])
        streams = joined

    plans = [reduce_order(count, m % 2 == 1) for m in range(micro_count)]
    batches = [list(range(micro_count))] if count * rows <= 128 else [[m] for m in range(micro_count)]
    outputs = []
    for batch in batches:
        results = run_experts(
            me_list,
            [streams[m] for m in batch],
            norm_gain.reshape(1, width),
            router_weight.T,
            jnp.concatenate([hot_all[m] for m in batch]),
            gate,
            up,
            down,
            gate_up_scale[0],
            down_scale,
            tuple(plans[m][1] for m in batch),
        )
        for m, (send, keep, own) in zip(batch, results):
            outputs.append(reduce_own(send, keep, own, plans[m][0], count))
    return jnp.stack(outputs)


def solution(mesh):
    in_specs = (
        P(None, ("groups", "expert"), None),
        P(None, ("groups", "expert"), None),
        P(None, ("groups", "expert"), None, None, None),
        P(None, ("groups", "expert")),
        P(None, ("groups", "expert"), None),
        P(None, "expert"),
        P(),
        P(),
        P("expert", None, None),
        P("expert", None, None),
        P("expert", None, None),
        P("expert", None, None, None),
        P("expert", None, None),
        P("expert", None),
    )
    out_specs = P(None, ("groups", "expert"), None)
    return jax.shard_map(body, mesh=mesh, in_specs=in_specs, out_specs=out_specs, check_vma=False)
```

```python
import functools

import jax
import jax.numpy as jnp
from jax import lax
from jax.experimental import pallas as pl
from jax.experimental.pallas import tpu as pltpu
from jax.sharding import PartitionSpec as P

LANES = 128
KV_HEADS = 4
HEAD_DIM = 128
MIB = 1 << 20


def attend_kernel(micro, span, kv_heads, len_ref, q_ref, kv_ref, out_ref, q_scr, o_scr):
    step = pl.program_id(0)
    rows, width = q_ref.shape
    heads = width // HEAD_DIM
    per_group = heads // kv_heads
    positions = kv_ref.shape[1]

    @pl.when(step == 0)
    def _():
        for h in range(heads):
            q_scr[h] = q_ref[:, h * HEAD_DIM : (h + 1) * HEAD_DIM].astype(jnp.float32)

    column = lax.broadcasted_iota(jnp.int32, (heads, 2 * positions), 1)
    is_key = column % 2 == 0
    blocks, weights = [], []
    for i in range(span):
        row = step * span + i
        parts = [
            kv_ref[i, :, :, g * HEAD_DIM : (g + 1) * HEAD_DIM].reshape(2 * positions, HEAD_DIM)
            for g in range(kv_heads)
        ]
        blocks.append(parts)
        scores = jnp.concatenate(
            [
                lax.dot_general(
                    q_scr[g * per_group : (g + 1) * per_group, row, :].astype(jnp.bfloat16),
                    parts[g],
                    (((1,), (1,)), ((), ())),
                    preferred_element_type=jnp.float32,
                )
                for g in range(kv_heads)
            ],
            axis=0,
        ) * HEAD_DIM ** (-0.5)
        visible = is_key & (column < 2 * len_ref[micro, row])
        scores = jnp.where(visible, scores, -1e30)
        raised = jnp.exp(scores - jnp.max(scores, axis=-1, keepdims=True))
        raised = raised / jnp.sum(raised, axis=-1, keepdims=True)
        weights.append(pltpu.roll(raised, 1, 1).astype(jnp.bfloat16))
    for i in range(span):
        row = step * span + i
        for g in range(kv_heads):
            o_scr[g * per_group : (g + 1) * per_group, row, :] = jnp.dot(
                weights[i][g * per_group : (g + 1) * per_group],
                blocks[i][g],
                preferred_element_type=jnp.float32,
            )

    @pl.when(step == pl.num_programs(0) - 1)
    def _():
        for h in range(heads):
            out_ref[:, h * HEAD_DIM : (h + 1) * HEAD_DIM] = o_scr[h].astype(jnp.bfloat16)


def attend(queries, kv_cache, lengths, micro):
    _, rows, width = queries.shape
    heads = width // HEAD_DIM
    span = 4 if rows % 4 == 0 else 1
    kv_shape = kv_cache.shape[2:]
    return pl.pallas_call(
        functools.partial(attend_kernel, micro, span, KV_HEADS),
        grid_spec=pltpu.PrefetchScalarGridSpec(
            num_scalar_prefetch=1,
            grid=(rows // span,),
            in_specs=[
                pl.BlockSpec((None, rows, width), lambda r, n: (micro, 0, 0)),
                pl.BlockSpec((None, span) + kv_shape, lambda r, n: (micro, r, 0, 0, 0)),
            ],
            out_specs=pl.BlockSpec((rows, width), lambda r, n: (0, 0)),
            scratch_shapes=[pltpu.VMEM((heads, rows, HEAD_DIM), jnp.float32)] * 2,
        ),
        out_shape=jax.ShapeDtypeStruct((rows, width), jnp.bfloat16),
        name="attend",
        compiler_params=pltpu.CompilerParams(vmem_limit_bytes=8 * MIB),
        cost_estimate=pl.CostEstimate(
            flops=rows * width * 4 * 256, bytes_accessed=rows << 18, transcendentals=0
        ),
    )(lengths, *(pltpu.with_memory_space_constraint(x, pltpu.HBM) for x in (queries, kv_cache)))


def expand_kernel(stacked, table_ref, code_ref, out_ref):
    rows, columns = code_ref.shape
    tile = 16
    tables = [jnp.broadcast_to(table_ref[i : i + 1], (tile, LANES)) for i in range(8)]

    def one(i, lane):
        at = pl.ds(pl.multiple_of(i * tile, tile), tile)
        codes = code_ref[at, lane * LANES : (lane + 1) * LANES]
        codes = codes.astype(jnp.float32).astype(jnp.int32)
        upper = codes >= LANES
        low = jnp.bitwise_and(codes, LANES - 1)

        def take(table):
            return jnp.take_along_axis(table, low, axis=1, mode="promise_in_bounds")

        for q in range(4):
            value = jnp.where(upper, take(tables[2 * q + 1]), take(tables[2 * q]))
            value = value.astype(jnp.bfloat16)
            if stacked:
                out_ref[q, at, lane * LANES : (lane + 1) * LANES] = value
            else:
                first = q * columns + lane * LANES
                out_ref[at, first : first + LANES] = value

    for lane in range(columns // LANES):

        def body(i, _, lane=lane):
            one(i, lane)
            return 0

        lax.fori_loop(0, rows // tile, body, 0, unroll=rows // tile if rows // tile <= 12 else 8)


def expand(table, codes, stacked, after=()):
    rows, columns = codes.shape
    if stacked:
        block = 512
        grid = (columns // block,)
        code_spec = pl.BlockSpec((rows, block), lambda b: (0, b))
        out_spec = pl.BlockSpec((4, rows, block), lambda b: (0, 0, b))
        out_shape = (4, rows, columns)
    else:
        block = 128
        grid = (rows // block,)
        code_spec = pl.BlockSpec((block, columns), lambda b: (b, 0))
        out_spec = pl.BlockSpec((block, 4 * columns), lambda b: (b, 0))
        out_shape = (rows, 4 * columns)
    out = pl.pallas_call(
        functools.partial(expand_kernel, stacked),
        grid=grid,
        in_specs=[pl.BlockSpec(table.shape, lambda b: (0, 0)), code_spec],
        out_specs=out_spec,
        out_shape=jax.ShapeDtypeStruct(out_shape, jnp.bfloat16),
        name="expand",
        compiler_params=pltpu.CompilerParams(vmem_limit_bytes=6 * MIB),
        cost_estimate=pl.CostEstimate(
            flops=rows * columns * 8000, bytes_accessed=10 * rows * columns, transcendentals=0
        ),
    )(tie(table, *after), pltpu.with_memory_space_constraint(codes, pltpu.HBM))
    return out.reshape(4 * rows, columns) if stacked else out


def project_kernel(masks, counts, block, me_ref, *refs):
    pieces, refs = refs[: len(masks)], refs[len(masks) :]
    weight_ref, hidden_ref = refs[:2]
    out_refs, acc_ref = refs[2:-1], refs[-1]
    depth = weight_ref.shape[0]
    for first in range(0, depth, block):
        at = slice(first, first + block)
        rows_in = jnp.concatenate([ref[:, :, at].reshape(-1, block) for ref in pieces], axis=0)
        product = jnp.dot(rows_in, weight_ref[at, :], preferred_element_type=jnp.float32)
        product = product.reshape(acc_ref.shape)
        acc_ref[...] = product if first == 0 else acc_ref[...] + product
    me = me_ref[0]
    entry = 0
    for mask_list, m in zip(masks, counts):
        for mask in mask_list:
            source = me ^ mask
            projected = acc_ref[entry].astype(jnp.bfloat16).astype(jnp.float32)
            out_refs[m][source] = (hidden_ref[source, m].astype(jnp.float32) + projected).astype(
                jnp.bfloat16
            )
            entry += 1


def project(me, gathered, out_weight, hidden_columns):
    pieces = [array for chain in gathered for array, _ in chain]
    masks = tuple(mask for chain in gathered for _, mask in chain)
    counts = tuple(m for m, chain in enumerate(gathered) for _ in chain)
    shards, micro_count, rows, columns = hidden_columns.shape
    depth = out_weight.shape[0]
    in_vmem = pl.BlockSpec(memory_space=pltpu.VMEM)
    held = [*pieces, out_weight, hidden_columns]
    if shards <= 16:
        held = [pltpu.with_memory_space_constraint(x, pltpu.VMEM) for x in held]
    return pl.pallas_call(
        functools.partial(project_kernel, masks, counts, 1024),
        in_specs=[pl.BlockSpec(memory_space=pltpu.SMEM)] + [in_vmem] * len(held),
        out_specs=[in_vmem] * micro_count,
        out_shape=[jax.ShapeDtypeStruct((shards, rows, columns), jnp.bfloat16)] * micro_count,
        scratch_shapes=[pltpu.VMEM((shards * micro_count, rows, columns), jnp.float32)],
        name="project",
        compiler_params=pltpu.CompilerParams(vmem_limit_bytes=(8 if shards <= 16 else 60) * MIB),
        cost_estimate=pl.CostEstimate(
            flops=2 * shards * micro_count * rows * depth * columns,
            bytes_accessed=2 * depth * columns,
            transcendentals=0,
        ),
    )(me, *held)


def experts_kernel(masks, counts, orders, me_ref, *refs):
    pieces, refs = refs[: len(masks)], refs[len(masks) :]
    gain_ref, router_ref, hot_ref, gate_ref, up_ref, down_ref, gu_scale_ref, down_scale_ref = refs[
        :8
    ]
    groups = len(orders)
    send_refs, keep_refs, own_refs = (
        refs[8 + i * groups : 8 + (i + 1) * groups] for i in range(3)
    )
    token_scr, weight_scr, acc_ref = refs[-3:]
    _, shards, rows, columns = pieces[0].shape
    total, width = token_scr.shape
    part = shards * rows
    hidden_units = gate_ref.shape[0]
    me = me_ref[0]
    nt = (((1,), (1,)), ((), ()))

    for m in range(groups):
        mine = [
            (ref, i, mask)
            for ref, mask_list, n in zip(pieces, masks, counts)
            if n == m
            for i, mask in enumerate(mask_list)
        ]
        squares = jnp.zeros((part, columns), jnp.float32)
        for ref, i, _ in mine:
            value = ref[i].reshape(part, columns).astype(jnp.float32)
            squares += value * value
        mean = jnp.sum(squares, axis=-1, keepdims=True) / width
        inverse = lax.rsqrt(mean + 1e-06)
        for ref, i, mask in mine:
            at = pl.ds(0, columns)
            if len(mine) > 1:
                at = pl.ds(pl.multiple_of((me ^ mask) * columns, columns), columns)
            value = ref[i].reshape(part, columns).astype(jnp.float32)
            own_refs[m][:, at] = ref[i, me]
            token_scr[m * part : (m + 1) * part, at] = (
                value * inverse * gain_ref[:, at]
            ).astype(jnp.bfloat16)
    logits = lax.dot_general(
        token_scr[...], router_ref[...], nt, preferred_element_type=jnp.float32
    )
    hot = hot_ref[...].astype(jnp.float32) > 0.5
    logits = jnp.where(hot, logits, -1e30)
    raised = jnp.where(hot, jnp.exp(logits - jnp.max(logits, axis=-1, keepdims=True)), 0.0)
    raised = raised / jnp.sum(raised, axis=-1, keepdims=True)
    column = lax.broadcasted_iota(jnp.int32, raised.shape, 1) == me
    weight = jnp.sum(jnp.where(column, raised, 0.0), axis=-1, keepdims=True)
    weight = weight.astype(jnp.bfloat16).astype(jnp.float32)
    weight_scr[...] = jnp.broadcast_to(weight, (total, LANES)).reshape(weight_scr.shape)

    block, piece = 256, 1024
    for f in range(hidden_units // block):
        units = slice(f * block, (f + 1) * block)
        tokens = token_scr[...]
        gate = lax.dot_general(tokens, gate_ref[units, :], nt, preferred_element_type=jnp.float32)
        up = lax.dot_general(tokens, up_ref[units, :], nt, preferred_element_type=jnp.float32)
        gate = gate * gu_scale_ref[0:1, units]
        up = up * gu_scale_ref[1:2, units]
        inner = (gate / (1.0 + jnp.exp(-gate)) * up).astype(jnp.bfloat16)
        for c in range(width // piece):
            at = slice(c * piece, (c + 1) * piece)
            product = jnp.dot(inner, down_ref[units, at], preferred_element_type=jnp.float32)
            product = product.reshape(groups * shards, rows, piece)
            if f == 0:
                acc_ref[:, :, at] = product
            else:
                acc_ref[:, :, at] += product

    half = shards // 2
    for m, order in enumerate(orders):
        for p, mask in enumerate(order):
            source = m * shards + (me ^ mask)
            value = (acc_ref[source] * down_scale_ref[...]).astype(jnp.bfloat16)
            value = (value.astype(jnp.float32) * weight_scr[source][:, 0:1]).astype(jnp.bfloat16)
            if p < half:
                keep_refs[m][p] = value
            else:
                send_refs[m][p - half] = value


def run_experts(me, streams, gain, router, hot, gate, up, down, gu_scale, down_scale, orders):
    pieces = [array for chain in streams for array, _ in chain]
    masks = tuple(mask for chain in streams for _, mask in chain)
    counts = tuple(m for m, chain in enumerate(streams) for _ in chain)
    groups = len(streams)
    _, shards, rows, _ = pieces[0].shape
    hidden_units, width = gate.shape
    total = groups * shards * rows
    half_shape = jax.ShapeDtypeStruct((shards // 2, rows, width), jnp.bfloat16)
    in_vmem = pl.BlockSpec(memory_space=pltpu.VMEM)
    held = [gate, up, down]
    if total <= 256:
        held = [pltpu.with_memory_space_constraint(w, pltpu.VMEM) for w in held]
        pieces = [pltpu.with_memory_space_constraint(w, pltpu.VMEM) for w in pieces]
    outs = pl.pallas_call(
        functools.partial(experts_kernel, masks, counts, orders),
        in_specs=[pl.BlockSpec(memory_space=pltpu.SMEM)] + [in_vmem] * (len(pieces) + 8),
        out_specs=[in_vmem] * (3 * groups),
        out_shape=[half_shape] * (2 * groups)
        + [jax.ShapeDtypeStruct((rows, width), jnp.bfloat16)] * groups,
        scratch_shapes=[
            pltpu.VMEM((total, width), jnp.bfloat16),
            pltpu.VMEM((groups * shards, rows, LANES), jnp.float32),
            pltpu.VMEM((groups * shards, rows, width), jnp.float32),
        ],
        name="experts",
        compiler_params=pltpu.CompilerParams(vmem_limit_bytes=(14 if total <= 256 else 62) * MIB),
        cost_estimate=pl.CostEstimate(
            flops=6 * total * width * hidden_units,
            bytes_accessed=6 * width * hidden_units,
            transcendentals=0,
        ),
    )(me, *pieces, gain, router, hot, *held, gu_scale, down_scale)
    return [tuple(outs[i * groups + m] for i in range(3)) for m in range(groups)]


def swap(value, bit, count):
    return lax.ppermute(value, "expert", [(i, i ^ bit) for i in range(count)])


def tie(value, *earlier):
    return lax.optimization_barrier((value,) + earlier)[0]


def gather_all(value, count):
    held, masks = value[None], (0,)
    for bit in [1 << b for b in reversed(range(count.bit_length() - 1))]:
        held = jnp.concatenate([held, swap(held, bit, count)])
        masks = masks + tuple(mask ^ bit for mask in masks)
    return [(held, masks)]


def gather_two(one, two, fillers):
    count = 16
    far_one, near_one = swap(one, 8, count), swap(one, 4, count)
    pair_two = jnp.stack([two, swap(two, 2, count)])
    far_two, near_two = swap(pair_two, 8, count), swap(pair_two, 4, count)
    both_one = swap(far_one, 4, count)
    four_one = jnp.stack([one, far_one, near_one, both_one])
    side_one = swap(four_one, 2, count)
    done = [fillers[0]((four_one, pair_two))]
    both_two = swap(tie(far_two, done[0]), 4, count)
    if len(fillers) > 1:
        done.append(fillers[1]((far_two, done[0])))
    chain_one = [(four_one, (0, 8, 4, 12)), (side_one, (2, 10, 6, 14))]
    chain_two = [(pair_two, (0, 2)), (far_two, (8, 10)), (near_two, (4, 6)), (both_two, (12, 14))]
    for chain in (chain_one, chain_two):
        for i, (held, masks) in enumerate(list(chain)):
            if i:
                held = tie(held, done[-1])
            chain.append((swap(held, 1, count), tuple(m ^ 1 for m in masks)))
    return [chain_one, chain_two], done


def reduce_order(count, flipped):
    bits = [1 << b for b in range(count.bit_length() - 1)]
    if flipped:
        bits = [bits[0]] + bits[2:] + [bits[1]]
    order = tuple(
        sum(bit for i, bit in enumerate(bits) if (p >> (len(bits) - 1 - i)) & 1)
        for p in range(count)
    )
    return bits, order


def reduce_own(send, keep, own, bits, count):
    for i, bit in enumerate(bits):
        other = swap(send, bit, count)
        half = keep.shape[0] // 2
        if half == 0:
            break
        add = lambda a, b: (a.astype(jnp.float32) + b.astype(jnp.float32)).astype(jnp.bfloat16)
        send, keep = add(keep[half:], other[half:]), add(keep[:half], other[:half])
    mixture = keep[0].astype(jnp.float32) + other[0].astype(jnp.float32)
    return (own.astype(jnp.float32) + mixture).astype(jnp.bfloat16)


def body(
    hidden,
    queries,
    kv_cache,
    lengths,
    routes,
    out_weight,
    norm_gain,
    router_weight,
    gate_codes,
    up_codes,
    down_codes,
    codebooks,
    gate_up_scale,
    down_scale,
):
    micro_count, rows, width = hidden.shape
    count = lax.axis_size("expert")
    me = lax.axis_index("expert").astype(jnp.int32)
    me_list = me.reshape(1)
    columns = out_weight.shape[1]
    hot = (routes[..., None] == jnp.arange(count, dtype=jnp.int32)).any(axis=2)
    lead = hidden.reshape(micro_count, rows, count, columns).transpose(2, 0, 1, 3)
    tail = jnp.broadcast_to(hot.astype(jnp.bfloat16)[None], (count,) + hot.shape)
    packed = lax.all_to_all(
        jnp.concatenate([lead, tail], axis=-1), "expert", split_axis=0, concat_axis=0, tiled=True
    )
    words = codebooks[0].astype(jnp.float32).transpose(0, 2, 1).reshape(3, 8, LANES)
    *tables, me_list, packed = lax.optimization_barrier(
        (words[0], words[1], words[2], me_list, packed)
    )
    hidden_columns = packed[..., :columns]
    hot_all = packed[..., columns:].transpose(1, 0, 2, 3).reshape(micro_count, count * rows, count)

    attended = [attend(queries, kv_cache, lengths, m) for m in range(micro_count)]
    make_gate = lambda after: expand(tables[0], gate_codes[0].T, True, after)
    make_up = lambda after: expand(tables[1], up_codes[0].T, True, after)
    make_down = lambda after: expand(tables[2], down_codes[0], False, after)
    if count == 16 and micro_count == 2:
        gathered, (gate, up) = gather_two(*attended, [make_gate, make_up])
        column_parts = project(me_list, gathered, out_weight, hidden_columns)
        streams, (down,) = gather_two(*column_parts, [make_down])
    else:
        gate, up, down = make_gate(()), make_up(()), make_down(())
        gathered = [gather_all(value, count) for value in attended]
        column_parts = project(me_list, gathered, out_weight, hidden_columns)
        streams = [gather_all(value, count) for value in column_parts]
    if columns % LANES:
        joined = []
        for ((held, masks),) in streams:
            place = jnp.asarray([masks.index(i) for i in range(count)], jnp.int32)
            held = held[place[jnp.arange(count, dtype=jnp.int32) ^ me]]
            held = held.transpose(1, 2, 0, 3).reshape(1, count, rows, width)
            joined.append([(held, (0,))])
        streams = joined

    plans = [reduce_order(count, m % 2 == 1) for m in range(micro_count)]
    batches = [list(range(micro_count))] if count * rows <= 128 else [[m] for m in range(micro_count)]
    outputs = []
    for batch in batches:
        results = run_experts(
            me_list,
            [streams[m] for m in batch],
            norm_gain.reshape(1, width),
            router_weight.T,
            jnp.concatenate([hot_all[m] for m in batch]),
            gate,
            up,
            down,
            gate_up_scale[0],
            down_scale,
            tuple(plans[m][1] for m in batch),
        )
        for m, (send, keep, own) in zip(batch, results):
            outputs.append(reduce_own(send, keep, own, plans[m][0], count))
    return jnp.stack(outputs)


def solution(mesh):
    in_specs = (
        P(None, ("groups", "expert"), None),
        P(None, ("groups", "expert"), None),
        P(None, ("groups", "expert"), None, None, None),
        P(None, ("groups", "expert")),
        P(None, ("groups", "expert"), None),
        P(None, "expert"),
        P(),
        P(),
        P("expert", None, None),
        P("expert", None, None),
        P("expert", None, None),
        P("expert", None, None, None),
        P("expert", None, None),
        P("expert", None),
    )
    out_specs = P(None, ("groups", "expert"), None)
    return jax.shard_map(body, mesh=mesh, in_specs=in_specs, out_specs=out_specs, check_vma=False)
```

```python
import functools

import jax
import jax.numpy as jnp
from jax import lax
from jax.experimental import pallas as pl
from jax.experimental.pallas import tpu as pltpu
from jax.sharding import PartitionSpec as P

LANES = 128
KV_HEADS = 4
HEAD_DIM = 128
MIB = 1 << 20


def attend_kernel(micro, span, kv_heads, len_ref, q_ref, kv_ref, out_ref, q_scr, o_scr):
    step = pl.program_id(0)
    rows, width = q_ref.shape
    heads = width // HEAD_DIM
    per_group = heads // kv_heads
    positions = kv_ref.shape[1]

    @pl.when(step == 0)
    def _():
        for h in range(heads):
            q_scr[h] = q_ref[:, h * HEAD_DIM : (h + 1) * HEAD_DIM].astype(jnp.float32)

    column = lax.broadcasted_iota(jnp.int32, (heads, 2 * positions), 1)
    is_key = column % 2 == 0
    blocks, weights = [], []
    for i in range(span):
        row = step * span + i
        parts = [
            kv_ref[i, :, :, g * HEAD_DIM : (g + 1) * HEAD_DIM].reshape(2 * positions, HEAD_DIM)
            for g in range(kv_heads)
        ]
        blocks.append(parts)
        scores = jnp.concatenate(
            [
                lax.dot_general(
                    q_scr[g * per_group : (g + 1) * per_group, row, :].astype(jnp.bfloat16),
                    parts[g],
                    (((1,), (1,)), ((), ())),
                    preferred_element_type=jnp.float32,
                )
                for g in range(kv_heads)
            ],
            axis=0,
        ) * HEAD_DIM ** (-0.5)
        visible = is_key & (column < 2 * len_ref[micro, row])
        scores = jnp.where(visible, scores, -1e30)
        raised = jnp.exp(scores - jnp.max(scores, axis=-1, keepdims=True))
        raised = raised / jnp.sum(raised, axis=-1, keepdims=True)
        weights.append(pltpu.roll(raised, 1, 1).astype(jnp.bfloat16))
    for i in range(span):
        row = step * span + i
        for g in range(kv_heads):
            o_scr[g * per_group : (g + 1) * per_group, row, :] = jnp.dot(
                weights[i][g * per_group : (g + 1) * per_group],
                blocks[i][g],
                preferred_element_type=jnp.float32,
            )

    @pl.when(step == pl.num_programs(0) - 1)
    def _():
        for h in range(heads):
            out_ref[:, h * HEAD_DIM : (h + 1) * HEAD_DIM] = o_scr[h].astype(jnp.bfloat16)


def attend(queries, kv_cache, lengths, micro):
    _, rows, width = queries.shape
    heads = width // HEAD_DIM
    span = 4 if rows % 4 == 0 else 1
    kv_shape = kv_cache.shape[2:]
    return pl.pallas_call(
        functools.partial(attend_kernel, micro, span, KV_HEADS),
        grid_spec=pltpu.PrefetchScalarGridSpec(
            num_scalar_prefetch=1,
            grid=(rows // span,),
            in_specs=[
                pl.BlockSpec((None, rows, width), lambda r, n: (micro, 0, 0)),
                pl.BlockSpec((None, span) + kv_shape, lambda r, n: (micro, r, 0, 0, 0)),
            ],
            out_specs=pl.BlockSpec((rows, width), lambda r, n: (0, 0)),
            scratch_shapes=[pltpu.VMEM((heads, rows, HEAD_DIM), jnp.float32)] * 2,
        ),
        out_shape=jax.ShapeDtypeStruct((rows, width), jnp.bfloat16),
        name="attend",
        compiler_params=pltpu.CompilerParams(vmem_limit_bytes=8 * MIB),
        cost_estimate=pl.CostEstimate(
            flops=rows * width * 4 * 256, bytes_accessed=rows << 18, transcendentals=0
        ),
    )(lengths, *(pltpu.with_memory_space_constraint(x, pltpu.HBM) for x in (queries, kv_cache)))


def expand_kernel(stacked, table_ref, code_ref, out_ref):
    rows, columns = code_ref.shape
    tile = 16
    tables = [jnp.broadcast_to(table_ref[i : i + 1], (tile, LANES)) for i in range(8)]

    def one(i, lane):
        at = pl.ds(pl.multiple_of(i * tile, tile), tile)
        codes = code_ref[at, lane * LANES : (lane + 1) * LANES]
        codes = codes.astype(jnp.float32).astype(jnp.int32)
        upper = codes >= LANES
        low = jnp.bitwise_and(codes, LANES - 1)

        def take(table):
            return jnp.take_along_axis(table, low, axis=1, mode="promise_in_bounds")

        for q in range(4):
            value = jnp.where(upper, take(tables[2 * q + 1]), take(tables[2 * q]))
            value = value.astype(jnp.bfloat16)
            if stacked:
                out_ref[q, at, lane * LANES : (lane + 1) * LANES] = value
            else:
                first = q * columns + lane * LANES
                out_ref[at, first : first + LANES] = value

    for lane in range(columns // LANES):

        def body(i, _, lane=lane):
            one(i, lane)
            return 0

        lax.fori_loop(0, rows // tile, body, 0, unroll=rows // tile if rows // tile <= 12 else 8)


def expand(table, codes, stacked, after=(), part=None):
    rows, columns = codes.shape
    skip = 0
    if stacked:
        block = 512
        grid = (columns // block,)
        code_spec = pl.BlockSpec((rows, block), lambda b: (0, b))
        out_spec = pl.BlockSpec((4, rows, block), lambda b: (0, 0, b))
        out_shape = (4, rows, columns)
    else:
        block = 128
        if part is not None:
            skip, rows = part[0] // block, part[1]
        grid = (rows // block,)
        code_spec = pl.BlockSpec((block, columns), lambda b: (b + skip, 0))
        out_spec = pl.BlockSpec((block, 4 * columns), lambda b: (b, 0))
        out_shape = (rows, 4 * columns)
    out = pl.pallas_call(
        functools.partial(expand_kernel, stacked),
        grid=grid,
        in_specs=[pl.BlockSpec(table.shape, lambda b: (0, 0)), code_spec],
        out_specs=out_spec,
        out_shape=jax.ShapeDtypeStruct(out_shape, jnp.bfloat16),
        name="expand",
        compiler_params=pltpu.CompilerParams(vmem_limit_bytes=6 * MIB),
        cost_estimate=pl.CostEstimate(
            flops=rows * columns * 8000, bytes_accessed=10 * rows * columns, transcendentals=0
        ),
    )(tie(table, *after), pltpu.with_memory_space_constraint(codes, pltpu.HBM))
    return out.reshape(4 * rows, columns) if stacked else out


def project_kernel(masks, counts, block, me_ref, *refs):
    pieces, refs = refs[: len(masks)], refs[len(masks) :]
    weight_ref, hidden_ref = refs[:2]
    out_refs, acc_ref = refs[2:-1], refs[-1]
    depth = weight_ref.shape[0]
    for first in range(0, depth, block):
        at = slice(first, first + block)
        rows_in = jnp.concatenate([ref[:, :, at].reshape(-1, block) for ref in pieces], axis=0)
        product = jnp.dot(rows_in, weight_ref[at, :], preferred_element_type=jnp.float32)
        product = product.reshape(acc_ref.shape)
        acc_ref[...] = product if first == 0 else acc_ref[...] + product
    me = me_ref[0]
    entry = 0
    for mask_list, m in zip(masks, counts):
        for mask in mask_list:
            source = me ^ mask
            projected = acc_ref[entry].astype(jnp.bfloat16).astype(jnp.float32)
            out_refs[m][source] = (hidden_ref[source, m].astype(jnp.float32) + projected).astype(
                jnp.bfloat16
            )
            entry += 1


def project(me, gathered, out_weight, hidden_columns):
    pieces = [array for chain in gathered for array, _ in chain]
    masks = tuple(mask for chain in gathered for _, mask in chain)
    counts = tuple(m for m, chain in enumerate(gathered) for _ in chain)
    shards, micro_count, rows, columns = hidden_columns.shape
    depth = out_weight.shape[0]
    in_vmem = pl.BlockSpec(memory_space=pltpu.VMEM)
    held = [*pieces, out_weight, hidden_columns]
    if shards <= 16:
        held = [pltpu.with_memory_space_constraint(x, pltpu.VMEM) for x in held]
    return pl.pallas_call(
        functools.partial(project_kernel, masks, counts, 1024),
        in_specs=[pl.BlockSpec(memory_space=pltpu.SMEM)] + [in_vmem] * len(held),
        out_specs=[in_vmem] * micro_count,
        out_shape=[jax.ShapeDtypeStruct((shards, rows, columns), jnp.bfloat16)] * micro_count,
        scratch_shapes=[pltpu.VMEM((shards * micro_count, rows, columns), jnp.float32)],
        name="project",
        compiler_params=pltpu.CompilerParams(vmem_limit_bytes=(8 if shards <= 16 else 60) * MIB),
        cost_estimate=pl.CostEstimate(
            flops=2 * shards * micro_count * rows * depth * columns,
            bytes_accessed=2 * depth * columns,
            transcendentals=0,
        ),
    )(me, *held)


def experts_kernel(masks, counts, orders, downs, me_ref, *refs):
    pieces, refs = refs[: len(masks)], refs[len(masks) :]
    gain_ref, router_ref, hot_ref, gate_ref, up_ref, gu_scale_ref, down_scale_ref = refs[:7]
    down_refs, refs = refs[7 : 7 + downs], refs[7 + downs :]
    groups = len(orders)
    send_refs, keep_refs, own_refs = (
        refs[i * groups : (i + 1) * groups] for i in range(3)
    )
    token_scr = refs[-1]
    _, shards, rows, columns = pieces[0].shape
    total, width = token_scr.shape
    part = shards * rows
    me = me_ref[0]
    nt = (((1,), (1,)), ((), ()))

    hots = []
    for m, order in enumerate(orders):
        places = [me ^ mask for mask in order]
        hots += [hot_ref[m, place].astype(jnp.float32) for place in places]
        mine = [
            (ref, i, mask)
            for ref, mask_list, n in zip(pieces, masks, counts)
            if n == m
            for i, mask in enumerate(mask_list)
        ]
        chunk = slice(m * part, (m + 1) * part)
        squares = jnp.zeros((part, columns), jnp.float32)
        for ref, i, mask in mine:
            at = pl.ds(0, columns)
            if len(mine) > 1:
                at = pl.ds(pl.multiple_of((me ^ mask) * columns, columns), columns)
            value = jnp.concatenate([ref[i, place].astype(jnp.float32) for place in places])
            own_refs[m][:, at] = ref[i, me]
            token_scr[chunk, at] = value.astype(jnp.bfloat16)
            squares += value * value
        mean = jnp.sum(squares, axis=-1, keepdims=True) / width
        inverse = lax.rsqrt(mean + 1e-06)
        for first in range(0, width, 256):
            at = slice(first, first + 256)
            value = token_scr[chunk, at].astype(jnp.float32)
            token_scr[chunk, at] = (value * inverse * gain_ref[:, at]).astype(jnp.bfloat16)
    logits = lax.dot_general(
        token_scr[...], router_ref[...], nt, preferred_element_type=jnp.float32
    )
    hot = jnp.concatenate(hots)[:, : logits.shape[1]] > 0.5
    logits = jnp.where(hot, logits, -1e30)
    raised = jnp.where(hot, jnp.exp(logits - jnp.max(logits, axis=-1, keepdims=True)), 0.0)
    raised = raised / jnp.sum(raised, axis=-1, keepdims=True)
    column = lax.broadcasted_iota(jnp.int32, raised.shape, 1) == me
    weight = jnp.sum(jnp.where(column, raised, 0.0), axis=-1, keepdims=True)
    weight = weight.astype(jnp.bfloat16).astype(jnp.float32)

    block, piece = 256, 512
    inner = []
    for first in range(0, gate_ref.shape[0], block):
        units = slice(first, first + block)
        tokens = token_scr[...]
        gate = lax.dot_general(tokens, gate_ref[units, :], nt, preferred_element_type=jnp.float32)
        up = lax.dot_general(tokens, up_ref[units, :], nt, preferred_element_type=jnp.float32)
        gate = gate * gu_scale_ref[0:1, units]
        up = up * gu_scale_ref[1:2, units]
        inner.append((gate / (1.0 + jnp.exp(-gate)) * up).astype(jnp.bfloat16))
    inner = jnp.concatenate(inner, axis=1)

    half = shards // 2
    for first in range(0, width, piece):
        at = slice(first, first + piece)
        product, begin = None, 0
        for down_ref in down_refs:
            end = begin + down_ref.shape[0]
            term = jnp.dot(
                inner[:, begin:end], down_ref[:, at], preferred_element_type=jnp.float32
            )
            product, begin = term if product is None else product + term, end
        product = (product * down_scale_ref[:, at]).astype(jnp.bfloat16).astype(jnp.float32)
        product = product * weight
        for m in range(groups):
            for p in range(shards):
                row = m * part + p * rows
                value = product[row : row + rows].astype(jnp.bfloat16)
                if p < half:
                    keep_refs[m][p, :, at] = value
                else:
                    send_refs[m][p - half, :, at] = value


def run_experts(me, streams, gain, router, hot, gate, up, down, gu_scale, down_scale, orders):
    pieces = [array for chain in streams for array, _ in chain]
    masks = tuple(mask for chain in streams for _, mask in chain)
    counts = tuple(m for m, chain in enumerate(streams) for _ in chain)
    groups = len(streams)
    _, shards, rows, _ = pieces[0].shape
    hidden_units, width = gate.shape
    total = groups * shards * rows
    half_shape = jax.ShapeDtypeStruct((shards // 2, rows, width), jnp.bfloat16)
    in_vmem = pl.BlockSpec(memory_space=pltpu.VMEM)
    held = [gate, up, *down]
    if total <= 256:
        held = [pltpu.with_memory_space_constraint(w, pltpu.VMEM) for w in held]
        pieces = [pltpu.with_memory_space_constraint(w, pltpu.VMEM) for w in pieces]
    outs = pl.pallas_call(
        functools.partial(experts_kernel, masks, counts, orders, len(down)),
        in_specs=[pl.BlockSpec(memory_space=pltpu.SMEM)] + [in_vmem] * (len(pieces) + 7 + len(down)),
        out_specs=[in_vmem] * (3 * groups),
        out_shape=[half_shape] * (2 * groups)
        + [jax.ShapeDtypeStruct((rows, width), jnp.bfloat16)] * groups,
        scratch_shapes=[pltpu.VMEM((total, width), jnp.bfloat16)],
        name="experts",
        compiler_params=pltpu.CompilerParams(vmem_limit_bytes=(14 if total <= 256 else 62) * MIB),
        cost_estimate=pl.CostEstimate(
            flops=6 * total * width * hidden_units,
            bytes_accessed=6 * width * hidden_units,
            transcendentals=0,
        ),
    )(me, *pieces, gain, router, hot, *held[:2], gu_scale, down_scale, *held[2:])
    return [tuple(outs[i * groups + m] for i in range(3)) for m in range(groups)]


def swap(value, bit, count):
    return lax.ppermute(value, "expert", [(i, i ^ bit) for i in range(count)])


def tie(value, *earlier):
    return lax.optimization_barrier((value,) + earlier)[0]


def gather_all(value, count):
    held, masks = value[None], (0,)
    for bit in [1 << b for b in reversed(range(count.bit_length() - 1))]:
        held = jnp.concatenate([held, swap(held, bit, count)])
        masks = masks + tuple(mask ^ bit for mask in masks)
    return [(held, masks)]


def gather_two(one, two, fillers):
    count = 16
    far_one, near_one = swap(one, 8, count), swap(one, 4, count)
    pair_two = jnp.stack([two, swap(two, 2, count)])
    far_two, near_two = swap(pair_two, 8, count), swap(pair_two, 4, count)
    both_one = swap(far_one, 4, count)
    four_one = jnp.stack([one, far_one, near_one, both_one])
    side_one = swap(four_one, 2, count)
    done = [fillers[0]((four_one, pair_two))]
    both_two = swap(tie(far_two, done[0]), 4, count)
    if len(fillers) > 1:
        done.append(fillers[1]((far_two, done[0])))
    chain_one = [(four_one, (0, 8, 4, 12)), (side_one, (2, 10, 6, 14))]
    chain_two = [(pair_two, (0, 2)), (far_two, (8, 10)), (near_two, (4, 6)), (both_two, (12, 14))]
    for chain in (chain_one, chain_two):
        for i, (held, masks) in enumerate(list(chain)):
            if i:
                held = tie(held, done[-1])
            chain.append((swap(held, 1, count), tuple(m ^ 1 for m in masks)))
    return [chain_one, chain_two], done


def reduce_order(count, flipped):
    bits = [1 << b for b in range(count.bit_length() - 1)]
    if flipped:
        bits = [bits[0]] + bits[2:] + [bits[1]]
    order = tuple(
        sum(bit for i, bit in enumerate(bits) if (p >> (len(bits) - 1 - i)) & 1)
        for p in range(count)
    )
    return bits, order


def reduce_own(send, keep, own, bits, count):
    for i, bit in enumerate(bits):
        other = swap(send, bit, count)
        half = keep.shape[0] // 2
        if half == 0:
            break
        add = lambda a, b: (a.astype(jnp.float32) + b.astype(jnp.float32)).astype(jnp.bfloat16)
        send, keep = add(keep[half:], other[half:]), add(keep[:half], other[:half])
    mixture = keep[0].astype(jnp.float32) + other[0].astype(jnp.float32)
    return (own.astype(jnp.float32) + mixture).astype(jnp.bfloat16)


def body(
    hidden,
    queries,
    kv_cache,
    lengths,
    routes,
    out_weight,
    norm_gain,
    router_weight,
    gate_codes,
    up_codes,
    down_codes,
    codebooks,
    gate_up_scale,
    down_scale,
):
    micro_count, rows, width = hidden.shape
    count = lax.axis_size("expert")
    me = lax.axis_index("expert").astype(jnp.int32)
    me_list = me.reshape(1)
    columns = out_weight.shape[1]
    hot = (routes[..., None] == jnp.arange(count, dtype=jnp.int32)).any(axis=2)
    lead = hidden.reshape(micro_count, rows, count, columns).transpose(2, 0, 1, 3)
    tail = jnp.broadcast_to(hot.astype(jnp.bfloat16)[None], (count,) + hot.shape)
    packed = lax.all_to_all(
        jnp.concatenate([lead, tail], axis=-1), "expert", split_axis=0, concat_axis=0, tiled=True
    )
    words = codebooks[0].astype(jnp.float32).transpose(0, 2, 1).reshape(3, 8, LANES)
    *tables, me_list, packed = lax.optimization_barrier(
        (words[0], words[1], words[2], me_list, packed)
    )
    hidden_columns = packed[..., :columns]
    hot_all = packed[..., columns:].transpose(1, 0, 2, 3)

    attended = [attend(queries, kv_cache, lengths, m) for m in range(micro_count)]
    make_gate = lambda after: expand(tables[0], gate_codes[0].T, True, after)
    make_up = lambda after: expand(tables[1], up_codes[0].T, True, after)
    units = down_codes.shape[1]
    make_down = [
        lambda after, part=part: expand(tables[2], down_codes[0], False, after, part)
        for part in ((0, 2 * units // 3), (2 * units // 3, units // 3))
    ]
    if count == 16 and micro_count == 2:
        gathered, (gate, up) = gather_two(*attended, [make_gate, make_up])
        column_parts = project(me_list, gathered, out_weight, hidden_columns)
        streams, down = gather_two(*column_parts, make_down)
    else:
        gate, up, down = make_gate(()), make_up(()), [make(()) for make in make_down]
        gathered = [gather_all(value, count) for value in attended]
        column_parts = project(me_list, gathered, out_weight, hidden_columns)
        streams = [gather_all(value, count) for value in column_parts]
    if columns % LANES:
        joined = []
        for ((held, masks),) in streams:
            place = jnp.asarray([masks.index(i) for i in range(count)], jnp.int32)
            held = held[place[jnp.arange(count, dtype=jnp.int32) ^ me]]
            held = held.transpose(1, 2, 0, 3).reshape(1, count, rows, width)
            joined.append([(held, (0,))])
        streams = joined

    plans = [reduce_order(count, m % 2 == 1) for m in range(micro_count)]
    batches = [list(range(micro_count))] if count * rows <= 128 else [[m] for m in range(micro_count)]
    outputs = []
    for batch in batches:
        results = run_experts(
            me_list,
            [streams[m] for m in batch],
            norm_gain.reshape(1, width),
            router_weight.T,
            hot_all[batch[0] : batch[-1] + 1],
            gate,
            up,
            down,
            gate_up_scale[0],
            down_scale,
            tuple(plans[m][1] for m in batch),
        )
        for m, (send, keep, own) in zip(batch, results):
            outputs.append(reduce_own(send, keep, own, plans[m][0], count))
    return jnp.stack(outputs)


def solution(mesh):
    in_specs = (
        P(None, ("groups", "expert"), None),
        P(None, ("groups", "expert"), None),
        P(None, ("groups", "expert"), None, None, None),
        P(None, ("groups", "expert")),
        P(None, ("groups", "expert"), None),
        P(None, "expert"),
        P(),
        P(),
        P("expert", None, None),
        P("expert", None, None),
        P("expert", None, None),
        P("expert", None, None, None),
        P("expert", None, None),
        P("expert", None),
    )
    out_specs = P(None, ("groups", "expert"), None)
    return jax.shard_map(body, mesh=mesh, in_specs=in_specs, out_specs=out_specs, check_vma=False)
```

```python
import functools

import jax
import jax.numpy as jnp
from jax import lax
from jax.experimental import pallas as pl
from jax.experimental.pallas import tpu as pltpu
from jax.sharding import PartitionSpec as P

LANES = 128
KV_HEADS = 4
HEAD_DIM = 128
MIB = 1 << 20


def attend_kernel(micro, span, kv_heads, len_ref, q_ref, kv_ref, out_ref, q_scr, o_scr):
    step = pl.program_id(0)
    rows, width = q_ref.shape
    heads = width // HEAD_DIM
    per_group = heads // kv_heads
    positions = kv_ref.shape[1]

    @pl.when(step == 0)
    def _():
        for h in range(heads):
            q_scr[h] = q_ref[:, h * HEAD_DIM : (h + 1) * HEAD_DIM].astype(jnp.float32)

    column = lax.broadcasted_iota(jnp.int32, (heads, 2 * positions), 1)
    is_key = column % 2 == 0
    blocks, weights = [], []
    for i in range(span):
        row = step * span + i
        parts = [
            kv_ref[i, :, :, g * HEAD_DIM : (g + 1) * HEAD_DIM].reshape(2 * positions, HEAD_DIM)
            for g in range(kv_heads)
        ]
        blocks.append(parts)
        scores = jnp.concatenate(
            [
                lax.dot_general(
                    q_scr[g * per_group : (g + 1) * per_group, row, :].astype(jnp.bfloat16),
                    parts[g],
                    (((1,), (1,)), ((), ())),
                    preferred_element_type=jnp.float32,
                )
                for g in range(kv_heads)
            ],
            axis=0,
        ) * HEAD_DIM ** (-0.5)
        visible = is_key & (column < 2 * len_ref[micro, row])
        scores = jnp.where(visible, scores, -1e30)
        raised = jnp.exp(scores - jnp.max(scores, axis=-1, keepdims=True))
        raised = raised / jnp.sum(raised, axis=-1, keepdims=True)
        weights.append(pltpu.roll(raised, 1, 1).astype(jnp.bfloat16))
    for i in range(span):
        row = step * span + i
        for g in range(kv_heads):
            o_scr[g * per_group : (g + 1) * per_group, row, :] = jnp.dot(
                weights[i][g * per_group : (g + 1) * per_group],
                blocks[i][g],
                preferred_element_type=jnp.float32,
            )

    @pl.when(step == pl.num_programs(0) - 1)
    def _():
        for h in range(heads):
            out_ref[:, h * HEAD_DIM : (h + 1) * HEAD_DIM] = o_scr[h].astype(jnp.bfloat16)


def attend(queries, kv_cache, lengths, micro):
    _, rows, width = queries.shape
    heads = width // HEAD_DIM
    span = 4 if rows % 4 == 0 else 1
    kv_shape = kv_cache.shape[2:]
    return pl.pallas_call(
        functools.partial(attend_kernel, micro, span, KV_HEADS),
        grid_spec=pltpu.PrefetchScalarGridSpec(
            num_scalar_prefetch=1,
            grid=(rows // span,),
            in_specs=[
                pl.BlockSpec((None, rows, width), lambda r, n: (micro, 0, 0)),
                pl.BlockSpec((None, span) + kv_shape, lambda r, n: (micro, r, 0, 0, 0)),
            ],
            out_specs=pl.BlockSpec((rows, width), lambda r, n: (0, 0)),
            scratch_shapes=[pltpu.VMEM((heads, rows, HEAD_DIM), jnp.float32)] * 2,
        ),
        out_shape=jax.ShapeDtypeStruct((rows, width), jnp.bfloat16),
        name="attend",
        compiler_params=pltpu.CompilerParams(vmem_limit_bytes=8 * MIB),
        cost_estimate=pl.CostEstimate(
            flops=rows * width * 4 * 256, bytes_accessed=rows << 18, transcendentals=0
        ),
    )(lengths, *(pltpu.with_memory_space_constraint(x, pltpu.HBM) for x in (queries, kv_cache)))


def expand_kernel(stacked, skip, table_ref, code_ref, out_ref):
    rows, columns = code_ref.shape
    tile = 16
    tables = [jnp.broadcast_to(table_ref[i : i + 1], (tile, LANES)) for i in range(8)]

    def one(row, lane):
        codes = code_ref[pl.ds(skip + row, tile), pl.ds(lane, LANES)]
        codes = codes.astype(jnp.float32).astype(jnp.int32)
        upper = codes >= LANES
        low = jnp.bitwise_and(codes, LANES - 1)
        at = pl.ds(row, tile)

        def take(table):
            return jnp.take_along_axis(table, low, axis=1, mode="promise_in_bounds")

        for q in range(4):
            value = jnp.where(upper, take(tables[2 * q + 1]), take(tables[2 * q]))
            value = value.astype(jnp.bfloat16)
            if stacked:
                out_ref[q, at, pl.ds(lane, LANES)] = value
            else:
                out_ref[at, pl.ds(q * columns + lane, LANES)] = value

    if stacked:
        steps = columns // LANES

        def body(k, _):
            for row in range(0, rows, tile):
                one(row, pl.multiple_of(k * LANES, LANES))
            return 0

    else:
        steps = out_ref.shape[0] // tile

        def body(k, _):
            for lane in range(0, columns, LANES):
                one(pl.multiple_of(k * tile, tile), lane)
            return 0

    lax.fori_loop(0, steps, body, 0, unroll=16)


def expand(table, codes, stacked, after=(), part=None):
    rows, columns = codes.shape
    skip, count = part or (0, rows)
    out_shape = (4, rows, columns) if stacked else (count, 4 * columns)
    in_vmem = pl.BlockSpec(memory_space=pltpu.VMEM)
    out = pl.pallas_call(
        functools.partial(expand_kernel, stacked, skip),
        in_specs=[in_vmem, in_vmem],
        out_specs=in_vmem,
        out_shape=jax.ShapeDtypeStruct(out_shape, jnp.bfloat16),
        name="expand",
        compiler_params=pltpu.CompilerParams(vmem_limit_bytes=12 * MIB),
        cost_estimate=pl.CostEstimate(
            flops=count * columns * 8000, bytes_accessed=10 * count * columns, transcendentals=0
        ),
    )(tie(table, *after), pltpu.with_memory_space_constraint(codes, pltpu.VMEM))
    return out.reshape(4 * rows, columns) if stacked else out


def project_kernel(masks, counts, block, me_ref, *refs):
    pieces, refs = refs[: len(masks)], refs[len(masks) :]
    weight_ref, hidden_ref = refs[:2]
    out_refs, acc_ref = refs[2:-1], refs[-1]
    depth = weight_ref.shape[0]
    for first in range(0, depth, block):
        at = slice(first, first + block)
        rows_in = jnp.concatenate([ref[:, :, at].reshape(-1, block) for ref in pieces], axis=0)
        product = jnp.dot(rows_in, weight_ref[at, :], preferred_element_type=jnp.float32)
        product = product.reshape(acc_ref.shape)
        acc_ref[...] = product if first == 0 else acc_ref[...] + product
    me = me_ref[0]
    entry = 0
    for mask_list, m in zip(masks, counts):
        for mask in mask_list:
            source = me ^ mask
            projected = acc_ref[entry].astype(jnp.bfloat16).astype(jnp.float32)
            out_refs[m][source] = (hidden_ref[source, m].astype(jnp.float32) + projected).astype(
                jnp.bfloat16
            )
            entry += 1


def project(me, gathered, out_weight, hidden_columns):
    pieces = [array for chain in gathered for array, _ in chain]
    masks = tuple(mask for chain in gathered for _, mask in chain)
    counts = tuple(m for m, chain in enumerate(gathered) for _ in chain)
    shards, micro_count, rows, columns = hidden_columns.shape
    depth = out_weight.shape[0]
    in_vmem = pl.BlockSpec(memory_space=pltpu.VMEM)
    held = [*pieces, out_weight, hidden_columns]
    if shards <= 16:
        held = [pltpu.with_memory_space_constraint(x, pltpu.VMEM) for x in held]
    return pl.pallas_call(
        functools.partial(project_kernel, masks, counts, 1024),
        in_specs=[pl.BlockSpec(memory_space=pltpu.SMEM)] + [in_vmem] * len(held),
        out_specs=[in_vmem] * micro_count,
        out_shape=[jax.ShapeDtypeStruct((shards, rows, columns), jnp.bfloat16)] * micro_count,
        scratch_shapes=[pltpu.VMEM((shards * micro_count, rows, columns), jnp.float32)],
        name="project",
        compiler_params=pltpu.CompilerParams(vmem_limit_bytes=(8 if shards <= 16 else 60) * MIB),
        cost_estimate=pl.CostEstimate(
            flops=2 * shards * micro_count * rows * depth * columns,
            bytes_accessed=2 * depth * columns,
            transcendentals=0,
        ),
    )(me, *held)


def experts_kernel(masks, counts, orders, downs, me_ref, *refs):
    pieces, refs = refs[: len(masks)], refs[len(masks) :]
    gain_ref, router_ref, hot_ref, gate_ref, up_ref, gu_scale_ref, down_scale_ref = refs[:7]
    down_refs, refs = refs[7 : 7 + downs], refs[7 + downs :]
    groups = len(orders)
    send_refs, keep_refs, own_refs = (
        refs[i * groups : (i + 1) * groups] for i in range(3)
    )
    token_scr = refs[-1]
    _, shards, rows, columns = pieces[0].shape
    total, width = token_scr.shape
    part = shards * rows
    me = me_ref[0]
    nt = (((1,), (1,)), ((), ()))

    hots = []
    for m, order in enumerate(orders):
        places = [me ^ mask for mask in order]
        hots += [hot_ref[m, place].astype(jnp.float32) for place in places]
        mine = [
            (ref, i, mask)
            for ref, mask_list, n in zip(pieces, masks, counts)
            if n == m
            for i, mask in enumerate(mask_list)
        ]
        chunk = slice(m * part, (m + 1) * part)
        squares = jnp.zeros((part, columns), jnp.float32)
        for ref, i, mask in mine:
            at = pl.ds(0, columns)
            if len(mine) > 1:
                at = pl.ds(pl.multiple_of((me ^ mask) * columns, columns), columns)
            value = jnp.concatenate([ref[i, place].astype(jnp.float32) for place in places])
            own_refs[m][:, at] = ref[i, me]
            token_scr[chunk, at] = value.astype(jnp.bfloat16)
            squares += value * value
        mean = jnp.sum(squares, axis=-1, keepdims=True) / width
        inverse = lax.rsqrt(mean + 1e-06)
        for first in range(0, width, 256):
            at = slice(first, first + 256)
            value = token_scr[chunk, at].astype(jnp.float32)
            token_scr[chunk, at] = (value * inverse * gain_ref[:, at]).astype(jnp.bfloat16)
    logits = lax.dot_general(
        token_scr[...], router_ref[...], nt, preferred_element_type=jnp.float32
    )
    hot = jnp.concatenate(hots)[:, : logits.shape[1]] > 0.5
    logits = jnp.where(hot, logits, -1e30)
    raised = jnp.where(hot, jnp.exp(logits - jnp.max(logits, axis=-1, keepdims=True)), 0.0)
    raised = raised / jnp.sum(raised, axis=-1, keepdims=True)
    column = lax.broadcasted_iota(jnp.int32, raised.shape, 1) == me
    weight = jnp.sum(jnp.where(column, raised, 0.0), axis=-1, keepdims=True)
    weight = weight.astype(jnp.bfloat16).astype(jnp.float32)

    block, piece = 256, 512
    inner = []
    for first in range(0, gate_ref.shape[0], block):
        units = slice(first, first + block)
        tokens = token_scr[...]
        gate = lax.dot_general(tokens, gate_ref[units, :], nt, preferred_element_type=jnp.float32)
        up = lax.dot_general(tokens, up_ref[units, :], nt, preferred_element_type=jnp.float32)
        gate = gate * gu_scale_ref[0:1, units]
        up = up * gu_scale_ref[1:2, units]
        inner.append((gate / (1.0 + jnp.exp(-gate)) * up).astype(jnp.bfloat16))
    inner = jnp.concatenate(inner, axis=1)

    half = shards // 2
    for first in range(0, width, piece):
        at = slice(first, first + piece)
        product, begin = None, 0
        for down_ref in down_refs:
            end = begin + down_ref.shape[0]
            term = jnp.dot(
                inner[:, begin:end], down_ref[:, at], preferred_element_type=jnp.float32
            )
            product, begin = term if product is None else product + term, end
        product = (product * down_scale_ref[:, at]).astype(jnp.bfloat16).astype(jnp.float32)
        product = product * weight
        for m in range(groups):
            for p in range(shards):
                row = m * part + p * rows
                value = product[row : row + rows].astype(jnp.bfloat16)
                if p < half:
                    keep_refs[m][p, :, at] = value
                else:
                    send_refs[m][p - half, :, at] = value


def run_experts(me, streams, gain, router, hot, gate, up, down, gu_scale, down_scale, orders):
    pieces = [array for chain in streams for array, _ in chain]
    masks = tuple(mask for chain in streams for _, mask in chain)
    counts = tuple(m for m, chain in enumerate(streams) for _ in chain)
    groups = len(streams)
    _, shards, rows, _ = pieces[0].shape
    hidden_units, width = gate.shape
    total = groups * shards * rows
    half_shape = jax.ShapeDtypeStruct((shards // 2, rows, width), jnp.bfloat16)
    in_vmem = pl.BlockSpec(memory_space=pltpu.VMEM)
    held = [gate, up, *down]
    if total <= 256:
        held = [pltpu.with_memory_space_constraint(w, pltpu.VMEM) for w in held]
        pieces = [pltpu.with_memory_space_constraint(w, pltpu.VMEM) for w in pieces]
    outs = pl.pallas_call(
        functools.partial(experts_kernel, masks, counts, orders, len(down)),
        in_specs=[pl.BlockSpec(memory_space=pltpu.SMEM)] + [in_vmem] * (len(pieces) + 7 + len(down)),
        out_specs=[in_vmem] * (3 * groups),
        out_shape=[half_shape] * (2 * groups)
        + [jax.ShapeDtypeStruct((rows, width), jnp.bfloat16)] * groups,
        scratch_shapes=[pltpu.VMEM((total, width), jnp.bfloat16)],
        name="experts",
        compiler_params=pltpu.CompilerParams(vmem_limit_bytes=(14 if total <= 256 else 62) * MIB),
        cost_estimate=pl.CostEstimate(
            flops=6 * total * width * hidden_units,
            bytes_accessed=6 * width * hidden_units,
            transcendentals=0,
        ),
    )(me, *pieces, gain, router, hot, *held[:2], gu_scale, down_scale, *held[2:])
    return [tuple(outs[i * groups + m] for i in range(3)) for m in range(groups)]


def swap(value, bit, count):
    return lax.ppermute(value, "expert", [(i, i ^ bit) for i in range(count)])


def tie(value, *earlier):
    return lax.optimization_barrier((value,) + earlier)[0]


def gather_all(value, count):
    held, masks = value[None], (0,)
    for bit in [1 << b for b in reversed(range(count.bit_length() - 1))]:
        held = jnp.concatenate([held, swap(held, bit, count)])
        masks = masks + tuple(mask ^ bit for mask in masks)
    return [(held, masks)]


def gather_two(one, two, fillers):
    count = 16
    far_one, near_one = swap(one, 8, count), swap(one, 4, count)
    pair_two = jnp.stack([two, swap(two, 2, count)])
    far_two, near_two = swap(pair_two, 8, count), swap(pair_two, 4, count)
    both_one = swap(far_one, 4, count)
    four_one = jnp.stack([one, far_one, near_one, both_one])
    side_one = swap(four_one, 2, count)
    done = [fillers[0]((four_one, pair_two))]
    both_two = swap(tie(far_two, done[0]), 4, count)
    if len(fillers) > 1:
        done.append(fillers[1]((far_two, done[0])))
    chain_one = [(four_one, (0, 8, 4, 12)), (side_one, (2, 10, 6, 14))]
    chain_two = [(pair_two, (0, 2)), (far_two, (8, 10)), (near_two, (4, 6)), (both_two, (12, 14))]
    for chain in (chain_one, chain_two):
        for i, (held, masks) in enumerate(list(chain)):
            if i:
                held = tie(held, done[-1])
            chain.append((swap(held, 1, count), tuple(m ^ 1 for m in masks)))
    return [chain_one, chain_two], done


def reduce_order(count, flipped):
    bits = [1 << b for b in range(count.bit_length() - 1)]
    if flipped:
        bits = [bits[0]] + bits[2:] + [bits[1]]
    order = tuple(
        sum(bit for i, bit in enumerate(bits) if (p >> (len(bits) - 1 - i)) & 1)
        for p in range(count)
    )
    return bits, order


def reduce_own(send, keep, own, bits, count):
    for i, bit in enumerate(bits):
        other = swap(send, bit, count)
        half = keep.shape[0] // 2
        if half == 0:
            break
        add = lambda a, b: (a.astype(jnp.float32) + b.astype(jnp.float32)).astype(jnp.bfloat16)
        send, keep = add(keep[half:], other[half:]), add(keep[:half], other[:half])
    mixture = keep[0].astype(jnp.float32) + other[0].astype(jnp.float32)
    return (own.astype(jnp.float32) + mixture).astype(jnp.bfloat16)


def body(
    hidden,
    queries,
    kv_cache,
    lengths,
    routes,
    out_weight,
    norm_gain,
    router_weight,
    gate_codes,
    up_codes,
    down_codes,
    codebooks,
    gate_up_scale,
    down_scale,
):
    micro_count, rows, width = hidden.shape
    count = lax.axis_size("expert")
    me = lax.axis_index("expert").astype(jnp.int32)
    me_list = me.reshape(1)
    columns = out_weight.shape[1]
    hot = (routes[..., None] == jnp.arange(count, dtype=jnp.int32)).any(axis=2)
    lead = hidden.reshape(micro_count, rows, count, columns).transpose(2, 0, 1, 3)
    tail = jnp.broadcast_to(hot.astype(jnp.bfloat16)[None], (count,) + hot.shape)
    packed = lax.all_to_all(
        jnp.concatenate([lead, tail], axis=-1), "expert", split_axis=0, concat_axis=0, tiled=True
    )
    words = codebooks[0].astype(jnp.float32).transpose(0, 2, 1).reshape(3, 8, LANES)
    *tables, me_list, packed = lax.optimization_barrier(
        (words[0], words[1], words[2], me_list, packed)
    )
    hidden_columns = packed[..., :columns]
    hot_all = packed[..., columns:].transpose(1, 0, 2, 3)

    attended = [attend(queries, kv_cache, lengths, m) for m in range(micro_count)]
    make_gate = lambda after: expand(tables[0], gate_codes[0].T, True, after)
    make_up = lambda after: expand(tables[1], up_codes[0].T, True, after)
    units = down_codes.shape[1]
    make_down = [
        lambda after, part=part: expand(tables[2], down_codes[0], False, after, part)
        for part in ((0, 2 * units // 3), (2 * units // 3, units // 3))
    ]
    if count == 16 and micro_count == 2:
        gathered, (gate, up) = gather_two(*attended, [make_gate, make_up])
        column_parts = project(me_list, gathered, out_weight, hidden_columns)
        streams, down = gather_two(*column_parts, make_down)
    else:
        gate, up, down = make_gate(()), make_up(()), [make(()) for make in make_down]
        gathered = [gather_all(value, count) for value in attended]
        column_parts = project(me_list, gathered, out_weight, hidden_columns)
        streams = [gather_all(value, count) for value in column_parts]
    if columns % LANES:
        joined = []
        for ((held, masks),) in streams:
            place = jnp.asarray([masks.index(i) for i in range(count)], jnp.int32)
            held = held[place[jnp.arange(count, dtype=jnp.int32) ^ me]]
            held = held.transpose(1, 2, 0, 3).reshape(1, count, rows, width)
            joined.append([(held, (0,))])
        streams = joined

    plans = [reduce_order(count, m % 2 == 1) for m in range(micro_count)]
    batches = [list(range(micro_count))] if count * rows <= 128 else [[m] for m in range(micro_count)]
    outputs = []
    for batch in batches:
        results = run_experts(
            me_list,
            [streams[m] for m in batch],
            norm_gain.reshape(1, width),
            router_weight.T,
            hot_all[batch[0] : batch[-1] + 1],
            gate,
            up,
            down,
            gate_up_scale[0],
            down_scale,
            tuple(plans[m][1] for m in batch),
        )
        for m, (send, keep, own) in zip(batch, results):
            outputs.append(reduce_own(send, keep, own, plans[m][0], count))
    return jnp.stack(outputs)


def solution(mesh):
    in_specs = (
        P(None, ("groups", "expert"), None),
        P(None, ("groups", "expert"), None),
        P(None, ("groups", "expert"), None, None, None),
        P(None, ("groups", "expert")),
        P(None, ("groups", "expert"), None),
        P(None, "expert"),
        P(),
        P(),
        P("expert", None, None),
        P("expert", None, None),
        P("expert", None, None),
        P("expert", None, None, None),
        P("expert", None, None),
        P("expert", None),
    )
    out_specs = P(None, ("groups", "expert"), None)
    return jax.shard_map(body, mesh=mesh, in_specs=in_specs, out_specs=out_specs, check_vma=False)
```

```python
import functools

import jax
import jax.numpy as jnp
from jax import lax
from jax.experimental import pallas as pl
from jax.experimental.pallas import tpu as pltpu
from jax.sharding import PartitionSpec as P

LANES = 128
KV_HEADS = 4
HEAD_DIM = 128
MIB = 1 << 20


def attend_kernel(micro, span, kv_heads, len_ref, q_ref, kv_ref, out_ref, q_scr, o_scr):
    step = pl.program_id(0)
    rows, width = q_ref.shape
    heads = width // HEAD_DIM
    per_group = heads // kv_heads
    positions = kv_ref.shape[1]

    @pl.when(step == 0)
    def _():
        for h in range(heads):
            q_scr[h] = q_ref[:, h * HEAD_DIM : (h + 1) * HEAD_DIM].astype(jnp.float32)

    column = lax.broadcasted_iota(jnp.int32, (heads, 2 * positions), 1)
    is_key = column % 2 == 0
    blocks, weights = [], []
    for i in range(span):
        row = step * span + i
        parts = [
            kv_ref[i, :, :, g * HEAD_DIM : (g + 1) * HEAD_DIM].reshape(2 * positions, HEAD_DIM)
            for g in range(kv_heads)
        ]
        blocks.append(parts)
        scores = jnp.concatenate(
            [
                lax.dot_general(
                    q_scr[g * per_group : (g + 1) * per_group, row, :].astype(jnp.bfloat16),
                    parts[g],
                    (((1,), (1,)), ((), ())),
                    preferred_element_type=jnp.float32,
                )
                for g in range(kv_heads)
            ],
            axis=0,
        ) * HEAD_DIM ** (-0.5)
        visible = is_key & (column < 2 * len_ref[micro, row])
        scores = jnp.where(visible, scores, -1e30)
        raised = jnp.exp(scores - jnp.max(scores, axis=-1, keepdims=True))
        raised = raised / jnp.sum(raised, axis=-1, keepdims=True)
        weights.append(pltpu.roll(raised, 1, 1).astype(jnp.bfloat16))
    for i in range(span):
        row = step * span + i
        for g in range(kv_heads):
            o_scr[g * per_group : (g + 1) * per_group, row, :] = jnp.dot(
                weights[i][g * per_group : (g + 1) * per_group],
                blocks[i][g],
                preferred_element_type=jnp.float32,
            )

    @pl.when(step == pl.num_programs(0) - 1)
    def _():
        for h in range(heads):
            out_ref[:, h * HEAD_DIM : (h + 1) * HEAD_DIM] = o_scr[h].astype(jnp.bfloat16)


def attend(queries, kv_cache, lengths, micro):
    _, rows, width = queries.shape
    heads = width // HEAD_DIM
    span = rows
    kv_shape = kv_cache.shape[2:]
    return pl.pallas_call(
        functools.partial(attend_kernel, micro, span, KV_HEADS),
        grid_spec=pltpu.PrefetchScalarGridSpec(
            num_scalar_prefetch=1,
            grid=(rows // span,),
            in_specs=[
                pl.BlockSpec((None, rows, width), lambda r, n: (micro, 0, 0)),
                pl.BlockSpec((None, span) + kv_shape, lambda r, n: (micro, r, 0, 0, 0)),
            ],
            out_specs=pl.BlockSpec((rows, width), lambda r, n: (0, 0)),
            scratch_shapes=[pltpu.VMEM((heads, rows, HEAD_DIM), jnp.float32)] * 2,
        ),
        out_shape=jax.ShapeDtypeStruct((rows, width), jnp.bfloat16),
        name="attend",
        compiler_params=pltpu.CompilerParams(vmem_limit_bytes=12 * MIB),
        cost_estimate=pl.CostEstimate(
            flops=rows * width * 4 * 256, bytes_accessed=rows << 18, transcendentals=0
        ),
    )(lengths, *(pltpu.with_memory_space_constraint(x, pltpu.HBM) for x in (queries, kv_cache)))


def expand_kernel(stacked, skip, table_ref, code_ref, out_ref):
    rows, columns = code_ref.shape
    tile = 16
    tables = [jnp.broadcast_to(table_ref[i : i + 1], (tile, LANES)) for i in range(8)]

    def one(row, lane):
        codes = code_ref[pl.ds(skip + row, tile), pl.ds(lane, LANES)]
        codes = codes.astype(jnp.float32).astype(jnp.int32)
        upper = codes >= LANES
        low = jnp.bitwise_and(codes, LANES - 1)
        at = pl.ds(row, tile)

        def take(table):
            return jnp.take_along_axis(table, low, axis=1, mode="promise_in_bounds")

        for q in range(4):
            value = jnp.where(upper, take(tables[2 * q + 1]), take(tables[2 * q]))
            value = value.astype(jnp.bfloat16)
            if stacked:
                out_ref[q, at, pl.ds(lane, LANES)] = value
            else:
                out_ref[at, pl.ds(q * columns + lane, LANES)] = value

    if stacked:
        steps = columns // LANES

        def body(k, _):
            for row in range(0, rows, tile):
                one(row, pl.multiple_of(k * LANES, LANES))
            return 0

    else:
        steps = out_ref.shape[0] // tile

        def body(k, _):
            for lane in range(0, columns, LANES):
                one(pl.multiple_of(k * tile, tile), lane)
            return 0

    lax.fori_loop(0, steps, body, 0, unroll=16)


def expand(table, codes, stacked, after=(), part=None):
    rows, columns = codes.shape
    skip, count = part or (0, rows)
    out_shape = (4, rows, columns) if stacked else (count, 4 * columns)
    in_vmem = pl.BlockSpec(memory_space=pltpu.VMEM)
    out = pl.pallas_call(
        functools.partial(expand_kernel, stacked, skip),
        in_specs=[in_vmem, in_vmem],
        out_specs=in_vmem,
        out_shape=jax.ShapeDtypeStruct(out_shape, jnp.bfloat16),
        name="expand",
        compiler_params=pltpu.CompilerParams(vmem_limit_bytes=12 * MIB),
        cost_estimate=pl.CostEstimate(
            flops=count * columns * 8000, bytes_accessed=10 * count * columns, transcendentals=0
        ),
    )(tie(table, *after), pltpu.with_memory_space_constraint(codes, pltpu.VMEM))
    return out.reshape(4 * rows, columns) if stacked else out


def project_kernel(masks, counts, block, me_ref, *refs):
    pieces, refs = refs[: len(masks)], refs[len(masks) :]
    weight_ref, hidden_ref = refs[:2]
    out_refs, acc_ref = refs[2:-1], refs[-1]
    depth = weight_ref.shape[0]
    for first in range(0, depth, block):
        at = slice(first, first + block)
        rows_in = jnp.concatenate([ref[:, :, at].reshape(-1, block) for ref in pieces], axis=0)
        product = jnp.dot(rows_in, weight_ref[at, :], preferred_element_type=jnp.float32)
        product = product.reshape(acc_ref.shape)
        acc_ref[...] = product if first == 0 else acc_ref[...] + product
    me = me_ref[0]
    entry = 0
    for mask_list, m in zip(masks, counts):
        for mask in mask_list:
            source = me ^ mask
            projected = acc_ref[entry].astype(jnp.bfloat16).astype(jnp.float32)
            out_refs[m][source] = (hidden_ref[source, m].astype(jnp.float32) + projected).astype(
                jnp.bfloat16
            )
            entry += 1


def project(me, gathered, out_weight, hidden_columns):
    pieces = [array for chain in gathered for array, _ in chain]
    masks = tuple(mask for chain in gathered for _, mask in chain)
    counts = tuple(m for m, chain in enumerate(gathered) for _ in chain)
    shards, micro_count, rows, columns = hidden_columns.shape
    depth = out_weight.shape[0]
    in_vmem = pl.BlockSpec(memory_space=pltpu.VMEM)
    held = [*pieces, out_weight, hidden_columns]
    if shards <= 16:
        held = [pltpu.with_memory_space_constraint(x, pltpu.VMEM) for x in held]
    return pl.pallas_call(
        functools.partial(project_kernel, masks, counts, 1024),
        in_specs=[pl.BlockSpec(memory_space=pltpu.SMEM)] + [in_vmem] * len(held),
        out_specs=[in_vmem] * micro_count,
        out_shape=[jax.ShapeDtypeStruct((shards, rows, columns), jnp.bfloat16)] * micro_count,
        scratch_shapes=[pltpu.VMEM((shards * micro_count, rows, columns), jnp.float32)],
        name="project",
        compiler_params=pltpu.CompilerParams(vmem_limit_bytes=(8 if shards <= 16 else 60) * MIB),
        cost_estimate=pl.CostEstimate(
            flops=2 * shards * micro_count * rows * depth * columns,
            bytes_accessed=2 * depth * columns,
            transcendentals=0,
        ),
    )(me, *held)


def experts_kernel(masks, counts, orders, downs, me_ref, *refs):
    pieces, refs = refs[: len(masks)], refs[len(masks) :]
    gain_ref, router_ref, hot_ref, gate_ref, up_ref, gu_scale_ref, down_scale_ref = refs[:7]
    down_refs, refs = refs[7 : 7 + downs], refs[7 + downs :]
    groups = len(orders)
    send_refs, keep_refs, own_refs = (
        refs[i * groups : (i + 1) * groups] for i in range(3)
    )
    token_scr = refs[-1]
    _, shards, rows, columns = pieces[0].shape
    total, width = token_scr.shape
    part = shards * rows
    me = me_ref[0]
    nt = (((1,), (1,)), ((), ()))

    hots = []
    for m, order in enumerate(orders):
        places = [me ^ mask for mask in order]
        hots += [hot_ref[m, place].astype(jnp.float32) for place in places]
        mine = [
            (ref, i, mask)
            for ref, mask_list, n in zip(pieces, masks, counts)
            if n == m
            for i, mask in enumerate(mask_list)
        ]
        chunk = slice(m * part, (m + 1) * part)
        squares = jnp.zeros((part, columns), jnp.float32)
        for ref, i, mask in mine:
            at = pl.ds(0, columns)
            if len(mine) > 1:
                at = pl.ds(pl.multiple_of((me ^ mask) * columns, columns), columns)
            value = jnp.concatenate([ref[i, place].astype(jnp.float32) for place in places])
            own_refs[m][:, at] = ref[i, me]
            token_scr[chunk, at] = value.astype(jnp.bfloat16)
            squares += value * value
        mean = jnp.sum(squares, axis=-1, keepdims=True) / width
        inverse = lax.rsqrt(mean + 1e-06)
        for first in range(0, width, 256):
            at = slice(first, first + 256)
            value = token_scr[chunk, at].astype(jnp.float32)
            token_scr[chunk, at] = (value * inverse * gain_ref[:, at]).astype(jnp.bfloat16)
    logits = lax.dot_general(
        token_scr[...], router_ref[...], nt, preferred_element_type=jnp.float32
    )
    hot = jnp.concatenate(hots)[:, : logits.shape[1]] > 0.5
    logits = jnp.where(hot, logits, -1e30)
    raised = jnp.where(hot, jnp.exp(logits - jnp.max(logits, axis=-1, keepdims=True)), 0.0)
    raised = raised / jnp.sum(raised, axis=-1, keepdims=True)
    column = lax.broadcasted_iota(jnp.int32, raised.shape, 1) == me
    weight = jnp.sum(jnp.where(column, raised, 0.0), axis=-1, keepdims=True)
    weight = weight.astype(jnp.bfloat16).astype(jnp.float32)

    block, piece = 256, 512
    inner = []
    for first in range(0, gate_ref.shape[0], block):
        units = slice(first, first + block)
        tokens = token_scr[...]
        gate = lax.dot_general(tokens, gate_ref[units, :], nt, preferred_element_type=jnp.float32)
        up = lax.dot_general(tokens, up_ref[units, :], nt, preferred_element_type=jnp.float32)
        gate = gate * gu_scale_ref[0:1, units]
        up = up * gu_scale_ref[1:2, units]
        inner.append((gate / (1.0 + jnp.exp(-gate)) * up).astype(jnp.bfloat16))
    inner = jnp.concatenate(inner, axis=1)

    half = shards // 2
    for first in range(0, width, piece):
        at = slice(first, first + piece)
        product, begin = None, 0
        for down_ref in down_refs:
            end = begin + down_ref.shape[0]
            term = jnp.dot(
                inner[:, begin:end], down_ref[:, at], preferred_element_type=jnp.float32
            )
            product, begin = term if product is None else product + term, end
        product = (product * down_scale_ref[:, at]).astype(jnp.bfloat16).astype(jnp.float32)
        product = product * weight
        for m in range(groups):
            for p in range(shards):
                row = m * part + p * rows
                value = product[row : row + rows].astype(jnp.bfloat16)
                if p < half:
                    keep_refs[m][p, :, at] = value
                else:
                    send_refs[m][p - half, :, at] = value


def run_experts(me, streams, gain, router, hot, gate, up, down, gu_scale, down_scale, orders):
    pieces = [array for chain in streams for array, _ in chain]
    masks = tuple(mask for chain in streams for _, mask in chain)
    counts = tuple(m for m, chain in enumerate(streams) for _ in chain)
    groups = len(streams)
    _, shards, rows, _ = pieces[0].shape
    hidden_units, width = gate.shape
    total = groups * shards * rows
    half_shape = jax.ShapeDtypeStruct((shards // 2, rows, width), jnp.bfloat16)
    in_vmem = pl.BlockSpec(memory_space=pltpu.VMEM)
    held = [gate, up, *down]
    if total <= 256:
        held = [pltpu.with_memory_space_constraint(w, pltpu.VMEM) for w in held]
        pieces = [pltpu.with_memory_space_constraint(w, pltpu.VMEM) for w in pieces]
    outs = pl.pallas_call(
        functools.partial(experts_kernel, masks, counts, orders, len(down)),
        in_specs=[pl.BlockSpec(memory_space=pltpu.SMEM)] + [in_vmem] * (len(pieces) + 7 + len(down)),
        out_specs=[in_vmem] * (3 * groups),
        out_shape=[half_shape] * (2 * groups)
        + [jax.ShapeDtypeStruct((rows, width), jnp.bfloat16)] * groups,
        scratch_shapes=[pltpu.VMEM((total, width), jnp.bfloat16)],
        name="experts",
        compiler_params=pltpu.CompilerParams(vmem_limit_bytes=(14 if total <= 256 else 62) * MIB),
        cost_estimate=pl.CostEstimate(
            flops=6 * total * width * hidden_units,
            bytes_accessed=6 * width * hidden_units,
            transcendentals=0,
        ),
    )(me, *pieces, gain, router, hot, *held[:2], gu_scale, down_scale, *held[2:])
    return [tuple(outs[i * groups + m] for i in range(3)) for m in range(groups)]


def swap(value, bit, count):
    return lax.ppermute(value, "expert", [(i, i ^ bit) for i in range(count)])


def tie(value, *earlier):
    return lax.optimization_barrier((value,) + earlier)[0]


def gather_all(value, count):
    held, masks = value[None], (0,)
    for bit in [1 << b for b in reversed(range(count.bit_length() - 1))]:
        held = jnp.concatenate([held, swap(held, bit, count)])
        masks = masks + tuple(mask ^ bit for mask in masks)
    return [(held, masks)]


def gather_two(one, two, fillers):
    count = 16
    far_one, near_one = swap(one, 8, count), swap(one, 4, count)
    pair_two = jnp.stack([two, swap(two, 2, count)])
    far_two, near_two = swap(pair_two, 8, count), swap(pair_two, 4, count)
    both_one = swap(far_one, 4, count)
    four_one = jnp.stack([one, far_one, near_one, both_one])
    side_one = swap(four_one, 2, count)
    done = [fillers[0]((four_one, pair_two))]
    both_two = swap(tie(far_two, done[0]), 4, count)
    if len(fillers) > 1:
        done.append(fillers[1]((far_two, done[0])))
    chain_one = [(four_one, (0, 8, 4, 12)), (side_one, (2, 10, 6, 14))]
    chain_two = [(pair_two, (0, 2)), (far_two, (8, 10)), (near_two, (4, 6)), (both_two, (12, 14))]
    for chain in (chain_one, chain_two):
        for i, (held, masks) in enumerate(list(chain)):
            if i:
                held = tie(held, done[-1])
            chain.append((swap(held, 1, count), tuple(m ^ 1 for m in masks)))
    return [chain_one, chain_two], done


def reduce_order(count, flipped):
    bits = [1 << b for b in range(count.bit_length() - 1)]
    if flipped:
        bits = [bits[0]] + bits[2:] + [bits[1]]
    order = tuple(
        sum(bit for i, bit in enumerate(bits) if (p >> (len(bits) - 1 - i)) & 1)
        for p in range(count)
    )
    return bits, order


def reduce_own(send, keep, own, bits, count):
    for i, bit in enumerate(bits):
        other = swap(send, bit, count)
        half = keep.shape[0] // 2
        if half == 0:
            break
        add = lambda a, b: (a.astype(jnp.float32) + b.astype(jnp.float32)).astype(jnp.bfloat16)
        send, keep = add(keep[half:], other[half:]), add(keep[:half], other[:half])
    mixture = keep[0].astype(jnp.float32) + other[0].astype(jnp.float32)
    return (own.astype(jnp.float32) + mixture).astype(jnp.bfloat16)


def body(
    hidden,
    queries,
    kv_cache,
    lengths,
    routes,
    out_weight,
    norm_gain,
    router_weight,
    gate_codes,
    up_codes,
    down_codes,
    codebooks,
    gate_up_scale,
    down_scale,
):
    micro_count, rows, width = hidden.shape
    count = lax.axis_size("expert")
    me = lax.axis_index("expert").astype(jnp.int32)
    me_list = me.reshape(1)
    columns = out_weight.shape[1]
    hot = (routes[..., None] == jnp.arange(count, dtype=jnp.int32)).any(axis=2)
    lead = hidden.reshape(micro_count, rows, count, columns).transpose(2, 0, 1, 3)
    tail = jnp.broadcast_to(hot.astype(jnp.bfloat16)[None], (count,) + hot.shape)
    packed = lax.all_to_all(
        jnp.concatenate([lead, tail], axis=-1), "expert", split_axis=0, concat_axis=0, tiled=True
    )
    words = codebooks[0].astype(jnp.float32).transpose(0, 2, 1).reshape(3, 8, LANES)
    *tables, me_list, packed = lax.optimization_barrier(
        (words[0], words[1], words[2], me_list, packed)
    )
    hidden_columns = packed[..., :columns]
    hot_all = packed[..., columns:].transpose(1, 0, 2, 3)

    attended = [attend(queries, kv_cache, lengths, m) for m in range(micro_count)]
    make_gate = lambda after: expand(tables[0], gate_codes[0].T, True, after)
    make_up = lambda after: expand(tables[1], up_codes[0].T, True, after)
    units = down_codes.shape[1]
    make_down = [
        lambda after, part=part: expand(tables[2], down_codes[0], False, after, part)
        for part in ((0, 2 * units // 3), (2 * units // 3, units // 3))
    ]
    if count == 16 and micro_count == 2:
        gathered, (gate, up) = gather_two(*attended, [make_gate, make_up])
        column_parts = project(me_list, gathered, out_weight, hidden_columns)
        streams, down = gather_two(*column_parts, make_down)
    else:
        gate, up, down = make_gate(()), make_up(()), [make(()) for make in make_down]
        gathered = [gather_all(value, count) for value in attended]
        column_parts = project(me_list, gathered, out_weight, hidden_columns)
        streams = [gather_all(value, count) for value in column_parts]
    if columns % LANES:
        joined = []
        for ((held, masks),) in streams:
            place = jnp.asarray([masks.index(i) for i in range(count)], jnp.int32)
            held = held[place[jnp.arange(count, dtype=jnp.int32) ^ me]]
            held = held.transpose(1, 2, 0, 3).reshape(1, count, rows, width)
            joined.append([(held, (0,))])
        streams = joined

    plans = [reduce_order(count, m % 2 == 1) for m in range(micro_count)]
    batches = [list(range(micro_count))] if count * rows <= 128 else [[m] for m in range(micro_count)]
    outputs = []
    for batch in batches:
        results = run_experts(
            me_list,
            [streams[m] for m in batch],
            norm_gain.reshape(1, width),
            router_weight.T,
            hot_all[batch[0] : batch[-1] + 1],
            gate,
            up,
            down,
            gate_up_scale[0],
            down_scale,
            tuple(plans[m][1] for m in batch),
        )
        for m, (send, keep, own) in zip(batch, results):
            outputs.append(reduce_own(send, keep, own, plans[m][0], count))
    return jnp.stack(outputs)


def solution(mesh):
    in_specs = (
        P(None, ("groups", "expert"), None),
        P(None, ("groups", "expert"), None),
        P(None, ("groups", "expert"), None, None, None),
        P(None, ("groups", "expert")),
        P(None, ("groups", "expert"), None),
        P(None, "expert"),
        P(),
        P(),
        P("expert", None, None),
        P("expert", None, None),
        P("expert", None, None),
        P("expert", None, None, None),
        P("expert", None, None),
        P("expert", None),
    )
    out_specs = P(None, ("groups", "expert"), None)
    return jax.shard_map(body, mesh=mesh, in_specs=in_specs, out_specs=out_specs, check_vma=False)
```
